128 devices in a mesh: grid: 32 (over y, x, z_hi), layer: 4 (over z_lo, core).
Axes of the slice: x: 4, y: 4, z: 4 (z_hi: 2, z_lo: 2; z = z_hi * 2 + z_lo), core: 2. Of those that a mesh axis runs over, the one named last changes fastest.
Arguments:
- a_blocks: bfloat16 [128, 28, 4096], P('grid', 'layer'), may hold values from -0.125 to 0.125
- a_cols: int32 [128, 28], P('grid', 'layer'), may hold values from 0 to 127, as said below
- p_blocks: bfloat16 [128, 28, 4096], P(('grid', 'layer')), may hold values from -6 to 6
- slots: int32 [128, 28, 28], P('grid', 'layer'), may hold values from 0 to 127, as said below
Outputs:
- c_blocks: bfloat16 [128, 128, 4096], P(('grid', 'layer'))
The draws below stay inside these ranges and needn't reach their ends.
Inputs may be any that keep to these rules, and one draw needn't show every extreme that they name: `a_cols`: position k of every row names a block row i of p_blocks with (i) modulo the number of devices along layer equal to k // 7. The 28 entries of slots[r, k] are all different; entries for different k of one row may repeat.
All inputs are finite; a program needn't handle non-finite values.
Results may differ from the reference program's by a relative error of at most 0.001.
Values may be sent and summed in bfloat16 or wider, within the bound.
A program may use at most 128 MiB of HBM per device.

```python
import jax
import jax.numpy as jnp
from jax import lax

BS = 64
KL = 7
PROLONG_BLOCKS = 28
PRODUCT_BLOCKS = 128
OPERATOR_BLOCKS = 28
TOTAL_ROWS = 128
NIB = 1
N_GRID = 32
N_LAYER = 4


def draw_a_cols(key, part):
    first_key, second_key = jax.random.split(jax.random.fold_in(key, 17))
    grid_pick = jax.random.randint(first_key, (TOTAL_ROWS, OPERATOR_BLOCKS), 0, N_GRID)
    offset = jax.random.randint(second_key, (TOTAL_ROWS, OPERATOR_BLOCKS), 0, NIB)
    layer_of = (jnp.arange(OPERATOR_BLOCKS, dtype=jnp.int32) // KL)[None, :]
    columns = (grid_pick * N_LAYER + layer_of) * NIB + offset
    columns = columns.at[0, 0].set(0)
    columns = columns.at[TOTAL_ROWS - 1, OPERATOR_BLOCKS - 1].set(TOTAL_ROWS - 1)
    return columns.astype(jnp.int32)


def draw_slots(key, part):
    score_key = jax.random.fold_in(key, 29)
    raw = jax.random.randint(score_key, (TOTAL_ROWS, OPERATOR_BLOCKS, PRODUCT_BLOCKS), 0, 2 ** 20)
    rank_scores = raw * PRODUCT_BLOCKS + jnp.arange(PRODUCT_BLOCKS, dtype=jnp.int32)[None, None, :]
    extra_credit = jnp.zeros((TOTAL_ROWS, OPERATOR_BLOCKS, PRODUCT_BLOCKS), jnp.int32)
    extra_credit = extra_credit.at[0, 0, 0].set(2 ** 28)
    extra_credit = extra_credit.at[0, 0, PRODUCT_BLOCKS - 1].set(2 ** 28)
    block_values, picked_entries = lax.top_k(rank_scores + extra_credit, PROLONG_BLOCKS)
    return picked_entries.astype(jnp.int32)


def shard_levels(key, shape, cuts, low, high):
    def one(dim, parts):
        heights = jax.random.uniform(jax.random.fold_in(jax.random.fold_in(key, 6), dim), (parts,), jnp.float32, low / len(cuts), high / len(cuts))
        return jnp.repeat(jnp.exp(heights), shape[dim] // parts).reshape((-1,) + (1,) * (len(shape) - dim - 1))

    factor_of = one(*cuts[0])
    for cut in cuts[1:]:
        factor_of = factor_of * one(*cut)
    return factor_of


def scatter_about(own_key, dims, deviation, bound, cuts=(), kind=jnp.bfloat16):
    array = jax.random.normal(own_key, dims, jnp.float32) * deviation
    if len(cuts) > 0:
        array = shard_levels(own_key, dims, cuts, -0.22, 0.18) * array
    return jnp.clip(array, min=-bound, max=bound).astype(kind)


def setup_inputs(seed: int = 0) -> dict:
    splits = jax.random.split(jax.random.key(seed), 5)
    return {
        "a_blocks": scatter_about(splits[0], (TOTAL_ROWS, OPERATOR_BLOCKS, BS * BS), (BS * OPERATOR_BLOCKS) ** -0.5, 0.125, ((0, 32), (1, 4))),
        "a_cols": draw_a_cols(jax.random.fold_in(splits[4], 71), 0),
        "p_blocks": scatter_about(splits[2], (TOTAL_ROWS, PROLONG_BLOCKS, BS * BS), 1.0, 6.0, ((0, 128),)),
        "slots": draw_slots(jax.random.fold_in(splits[4], 71), 0),
    }


def reference(a_blocks, a_cols, p_blocks, slots):
    def one_row(items):
        a_row, col_row, slot_row = items
        left = a_row.astype(jnp.float32).reshape(OPERATOR_BLOCKS, BS, BS)
        right = jnp.take(p_blocks, col_row, axis=0).astype(jnp.float32).reshape(OPERATOR_BLOCKS, PROLONG_BLOCKS, BS, BS)
        product = jnp.einsum("kab,kmbc->kmac", left, right, precision=lax.Precision.HIGHEST)
        return jax.ops.segment_sum(product.reshape(OPERATOR_BLOCKS * PROLONG_BLOCKS, BS * BS), slot_row.reshape(-1), num_segments=PRODUCT_BLOCKS)

    summed = lax.map(one_row, (a_blocks, a_cols, slots))
    return summed.astype(jnp.bfloat16)
```

```python
import jax
import jax.numpy as jnp
from jax import lax
from jax.experimental import pallas as pl
from jax.experimental.pallas import tpu as pltpu
from jax.sharding import PartitionSpec as P

MESH = pl.DeviceIdType.MESH
ROWS = 112
ALL, LO, HI = (0, 4), (0, 2), (2, 4)
LANE_OF = {0: 0, -1: 1, 1: 2, 2: 3}


def place():
    g, l = lax.axis_index("grid"), lax.axis_index("layer")
    return g // 8, (g // 2) % 4, (g % 2) * 4 + l


def dev(y, x, j):
    return ((y * 4 + x) * 2 + j // 4, j % 4)


def m4(v):
    return lax.rem(v + 4, 4)


def kernel(
    src, a_src, slot_src, col_src, out,
    pall, abuf, sbuf, cbuf, csm, prod_hi, prod_lo, obuf,
    zs, zr, as_, ar, is_, ir, cs, cr, ls, ss, rs, os, orr, smem_sem,
):
    y, x, j = place()
    q = y * 4 + x
    barrier = pltpu.get_barrier_semaphore()
    peers = [dev(y, x, lax.rem(j + d, 8)) for d in range(1, 8)]
    peers += [
        dev(y, m4(x + 1), j), dev(y, m4(x - 1), j),
        dev(m4(y + 1), x, j), dev(m4(y - 1), x, j),
    ]
    for p in peers:
        pl.semaphore_signal(barrier, inc=1, device_id=p, device_id_type=MESH)
    pl.semaphore_wait(barrier, len(peers))

    def remote(s, d, ssem, rsem, to):
        return pltpu.make_async_remote_copy(
            src_ref=s, dst_ref=d, send_sem=ssem, recv_sem=rsem, device_id=to, device_id_type=MESH
        )

    half, layer = j // 4, j % 4
    own = [
        pltpu.make_async_copy(src.at[j], pall.at[q, j], ls.at[0]),
        pltpu.make_async_copy(a_src, abuf.at[layer, pl.ds(half * 4, 4)], ls.at[1]),
        pltpu.make_async_copy(slot_src, sbuf.at[layer, pl.ds(half * 4, 4)], ls.at[2]),
        pltpu.make_async_copy(col_src, cbuf.at[layer, half], ls.at[3]),
    ]
    for c in own:
        c.start()
    column = []
    for d in range(1, 8):
        t = lax.rem(j + d, 8)
        c = remote(src.at[t], pall.at[q, j], zs.at[d], zr.at[d], dev(y, x, t))
        c.start()
        column.append(c)
    later = []
    for d in range(1, 8):
        to = dev(y, x, lax.rem(j + d, 8))
        later += [
            remote(slot_src, sbuf.at[layer, pl.ds(half * 4, 4)], is_.at[d], ir.at[d], to),
            remote(col_src, cbuf.at[layer, half], cs.at[d], cr.at[d], to),
            remote(a_src, abuf.at[layer, pl.ds(half * 4, 4)], as_.at[d], ar.at[d], to),
        ]
    for c in own:
        c.wait()
    for c in column:
        c.wait_recv()

    sent = []

    def block(h, ident, aoff, boff, rows, axis, step):
        if h == 0:
            bx, by = m4(x + aoff), m4(y + boff)
        else:
            by, bx = m4(y + aoff), m4(x + boff)
        if (axis == "a") == (h == 0):
            to = dev(y, m4(x + step), j)
        else:
            to = dev(m4(y + step), x, j)
        ref = pall.at[by * 4 + bx, pl.ds(4 * h + rows[0], rows[1] - rows[0])]
        return remote(ref, ref, ss.at[h, ident], rs.at[h, ident], to)

    def send(*args):
        c = block(*args)
        c.start()
        sent.append(c)

    def recv(h, ident, aoff, boff, rows):
        block(h, ident, aoff, boff, rows, "a", 1).wait_recv()

    for h in (0, 1):
        send(h, 0, 0, 0, ALL, "a", 1)
        send(h, 1, 0, 0, ALL, "a", -1)
    for h in (0, 1):
        send(h, 4, 0, 0, ALL, "b", 1)
        send(h, 5, 0, 0, ALL, "b", -1)
    for c in later:
        c.start()
    for h in (0, 1):
        recv(h, 0, -1, 0, ALL)
        send(h, 2, -1, 0, LO, "a", 1)
        send(h, 6, -1, 0, ALL, "b", 1)
        send(h, 7, -1, 0, ALL, "b", -1)
        recv(h, 1, 1, 0, ALL)
        send(h, 3, 1, 0, HI, "a", -1)
        send(h, 8, 1, 0, ALL, "b", 1)
        send(h, 9, 1, 0, ALL, "b", -1)

    def onward(aoff):
        i = LANE_OF[aoff]
        for h in (0, 1):
            recv(h, 4 + 2 * i, aoff, -1, ALL)
            send(h, 12 + 2 * i, aoff, -1, LO, "b", 1)
            recv(h, 5 + 2 * i, aoff, 1, ALL)
            send(h, 13 + 2 * i, aoff, 1, HI, "b", -1)

    onward(0)
    for h in (0, 1):
        recv(h, 2, 2, 0, LO)
        recv(h, 3, 2, 0, HI)
        send(h, 10, 2, 0, ALL, "b", 1)
        send(h, 11, 2, 0, ALL, "b", -1)
    onward(-1)
    onward(1)
    onward(2)

    for c in later:
        c.wait_recv()
    cols = pltpu.make_async_copy(cbuf, csm, smem_sem)
    cols.start()
    for l in range(4):
        base = l * 256 + 224
        prod_hi[base : base + 32, :] = jnp.zeros((32, 512), jnp.bfloat16)
        prod_lo[base : base + 32, :] = jnp.zeros((32, 512), jnp.bfloat16)
    cols.wait()

    for h in (0, 1):
        for aoff in (0, -1, 1, 2):
            i = LANE_OF[aoff]
            recv(h, 12 + 2 * i, aoff, 2, LO)
            recv(h, 13 + 2 * i, aoff, 2, HI)

    left = lax.broadcasted_iota(jnp.int32, (64, 128), 1) < 64
    target = lax.broadcasted_iota(jnp.int32, (128, 256), 0)

    def row_product(r):
        def one_layer(l, carry):
            for kk in range(7):
                col = csm[l, r // 4, r % 4, kk]
                block_p = pall[col // 8, col % 8]
                even_odd = abuf[l, r, kk]
                odd_even = jnp.concatenate([even_odd[:, 64:], even_odd[:, :64]], axis=1)
                zero = jnp.zeros((64, 128), jnp.bfloat16)
                weights = jnp.concatenate(
                    [
                        jnp.where(left, jnp.concatenate([even_odd, odd_even], axis=0), zero),
                        jnp.where(left, zero, jnp.concatenate([odd_even, even_odd], axis=0)),
                    ],
                    axis=0,
                )
                prod = lax.dot_general(
                    block_p, weights, (((1,), (1,)), ((), ())), preferred_element_type=jnp.float32
                )
                moved = pltpu.roll(prod, ROWS - 4, 0)
                base = pl.multiple_of(l * 256 + kk * 32, 32)
                for cp in range(4):
                    part = prod[28 * cp : 28 * cp + 32] if cp % 2 == 0 else moved[28 * cp - 4 : 28 * cp + 28]
                    hi = part.astype(jnp.bfloat16)
                    lo = (part - hi.astype(jnp.float32)).astype(jnp.bfloat16)
                    prod_hi[pl.ds(base, 32), cp * 128 : cp * 128 + 128] = hi
                    prod_lo[pl.ds(base, 32), cp * 128 : cp * 128 + 128] = lo
            return carry

        lax.fori_loop(0, 4, one_layer, 0)
        total = jnp.zeros((128, 512), jnp.float32)
        for l in range(4):
            s = sbuf[l, r]
            lanes = jnp.concatenate([s[0:1], s[1:2]], axis=1)
            chosen = jnp.where(lanes == target, 1.0, 0.0).astype(jnp.bfloat16)
            total += jnp.dot(chosen, prod_hi[l * 256 : l * 256 + 256], preferred_element_type=jnp.float32)
            total += jnp.dot(chosen, prod_lo[l * 256 : l * 256 + 256], preferred_element_type=jnp.float32)
        return total.astype(jnp.bfloat16)

    def give(d, r):
        return remote(obuf.at[d], out.at[j], os.at[d], orr.at[d], dev(y, x, r))

    def one_row(d, carry):
        r = lax.rem(j + d, 8)
        obuf[d] = row_product(r)
        give(d, r).start()
        return carry

    lax.fori_loop(1, 8, one_row, 0)
    out[j] = row_product(j)

    for c in column + later + sent:
        c.wait_send()
    for d in range(1, 8):
        give(d, lax.rem(j + d, 8)).wait()


def per_device(a_blocks, a_cols, p_blocks, slots):
    pt = p_blocks.reshape(28, 64, 8, 4, 2).transpose(2, 3, 0, 4, 1).reshape(8, ROWS, 128)
    a = a_blocks.reshape(4, 7, 32, 128)
    s = jnp.pad(slots, ((0, 0), (0, 1), (0, 4)), constant_values=-1).reshape(4, 2, 128)
    s = jnp.pad(s, ((0, 0), (0, 6), (0, 0)), constant_values=-1)
    cols = jnp.pad(a_cols, ((0, 0), (0, 121)))
    dma = pltpu.SemaphoreType.DMA
    any_ = pl.BlockSpec(memory_space=pl.ANY)
    got = pl.pallas_call(
        kernel,
        out_shape=jax.ShapeDtypeStruct((8, 128, 512), jnp.bfloat16),
        in_specs=[any_, any_, any_, any_],
        out_specs=pl.BlockSpec(memory_space=pltpu.VMEM),
        scratch_shapes=[
            pltpu.VMEM((16, 8, ROWS, 128), jnp.bfloat16),
            pltpu.VMEM((4, 8, 7, 32, 128), jnp.bfloat16),
            pltpu.VMEM((4, 8, 8, 128), jnp.int32),
            pltpu.VMEM((4, 2, 4, 128), jnp.int32),
            pltpu.SMEM((4, 2, 4, 128), jnp.int32),
            pltpu.VMEM((1024, 512), jnp.bfloat16),
            pltpu.VMEM((1024, 512), jnp.bfloat16),
            pltpu.VMEM((8, 128, 512), jnp.bfloat16),
            dma((8,)), dma((8,)), dma((8,)), dma((8,)), dma((8,)), dma((8,)), dma((8,)), dma((8,)),
            dma((4,)), dma((2, 20)), dma((2, 20)), dma((8,)), dma((8,)), dma,
        ],
        compiler_params=pltpu.CompilerParams(
            collective_id=0, has_side_effects=True, vmem_limit_bytes=40 * 2**20
        ),
        name="column_split",
    )(pt, a, s, cols)
    got = got.reshape(8, 128, 4, 2, 2, 32).transpose(1, 5, 4, 0, 2, 3)
    return got.reshape(1, 128, 4096)


def solution(mesh):
    placed = (
        P("grid", "layer", None),
        P("grid", "layer"),
        P(("grid", "layer"), None, None),
        P("grid", "layer", None),
    )
    return jax.shard_map(
        per_device,
        mesh=mesh,
        in_specs=placed,
        out_specs=P(("grid", "layer"), None, None),
        check_vma=False,
    )
```

```python
import jax
import jax.numpy as jnp
from jax import lax
from jax.experimental import pallas as pl
from jax.experimental.pallas import tpu as pltpu
from jax.sharding import PartitionSpec as P

MESH = pl.DeviceIdType.MESH
ROWS = 112
ALL, LO, HI = (0, 2), (0, 1), (1, 1)
ORDER = {0: 0, -1: 1, 1: 2, 2: 3}
QUARTERS = (0, 1, 3, 2)


def place():
    g, l = lax.axis_index("grid"), lax.axis_index("layer")
    return g // 8, (g // 2) % 4, (g % 2) * 4 + l


def dev(y, x, j):
    return ((y * 4 + x) * 2 + j // 4, j % 4)


def m4(v):
    return lax.rem(v + 4, 4)


def columns_out(tiles):
    lane = lax.broadcasted_iota(jnp.int32, tiles[0].shape, 1)
    for i in range(5):
        d, up = 2 << i, (lane & (2 << i)) != 0
        swapped = list(tiles)
        for t in range(32):
            if not t & (1 << i):
                low, high = tiles[t], tiles[t | (1 << i)]
                swapped[t] = jnp.where(up, pltpu.roll(high, d, 1), low)
                swapped[t | (1 << i)] = jnp.where(up, high, pltpu.roll(low, 128 - d, 1))
        tiles = swapped
    top, bottom = (lane & 64) != 0, (lane & 1) != 0
    done = []
    for v in tiles:
        moved = jnp.where(top, pltpu.roll(v, 63, 1), pltpu.roll(v, 65, 1))
        done.append(jnp.where(top == bottom, v, moved))
    return done


def kernel(
    p_raw, a_raw, slot_raw, col_src, out,
    praw, araw, sraw, pf, pt, af, amine, imine,
    pall, abuf, ibuf, cbuf, csm, wbuf, oh, prod_hi, prod_lo, obuf,
    ls, zs, zr, as_, ar, is_, ir, cs, cr, ss, rs, rl_, os, orr, smem_sem,
):
    y, x, j = place()
    q, z, core = y * 4 + x, j // 2, j % 2
    half, layer = j // 4, j % 4
    part_of_j = layer * 2 + half
    partner = j + 1 - 2 * core
    xs = {0: x, 1: m4(x + 1), 2: m4(x + 2), -1: m4(x - 1)}
    ys = {0: y, 1: m4(y + 1), 2: m4(y + 2), -1: m4(y - 1)}
    beside = {(0, 1): dev(y, xs[1], j), (0, -1): dev(y, xs[-1], j), (1, 1): dev(ys[1], x, j), (1, -1): dev(ys[-1], x, j)}
    chip = {e: m4(z + e) for e in range(4)}

    def in_column(t):
        return (q * 2 + t // 4, t % 4)

    targets = [in_column(lax.rem(j + d, 8)) for d in range(1, 8)]
    barrier = pltpu.get_barrier_semaphore()
    for to in targets + list(beside.values()):
        pl.semaphore_signal(barrier, inc=1, device_id=to, device_id_type=MESH)
    loads = [
        pltpu.make_async_copy(p_raw, praw, ls.at[0]),
        pltpu.make_async_copy(a_raw, araw, ls.at[1]),
        pltpu.make_async_copy(slot_raw, sraw, ls.at[2]),
        pltpu.make_async_copy(col_src, cbuf.at[part_of_j], ls.at[3]),
    ]
    for c in loads:
        c.start()

    def remote(s, d, ssem, rsem, to):
        return pltpu.make_async_remote_copy(
            src_ref=s, dst_ref=d, send_sem=ssem, recv_sem=rsem, device_id=to, device_id_type=MESH
        )

    def take(ref, sem):
        pltpu.make_async_copy(ref, ref, sem).wait()

    loads[0].wait()
    for m in (0, 8, 16, 24):
        rows = min(8, 28 - m)
        tiles = []
        for t in range(32):
            v = praw[m : m + rows, t * 128 : t * 128 + 128].astype(jnp.float32)
            tiles.append(v if rows == 8 else jnp.concatenate([v, v], axis=0))
        for t, v in enumerate(columns_out(tiles)):
            at = (t % 4) * 28 + m
            pf[t // 4, at : at + rows, :] = v[:rows]
    for t in range(8):
        pt[t] = pf[t].astype(jnp.bfloat16)
    pall[q, j] = pt[j]
    pl.semaphore_wait(barrier, 11)

    remote(pt.at[partner], pall.at[q, j], zs, zr.at[0], in_column(partner)).start()
    for e in (1, 3, 2):
        for c in (0, 1):
            t = 2 * m4(z - e) + c
            remote(pt.at[t], pall.at[q, j], zs, zr.at[e], in_column(t)).start()

    def lead(e):
        return 0 if e in (0, 3) else 1

    def spot(e, aoff, boff, rows):
        if lead(e) == 0:
            n = ys[boff] * 4 + xs[aoff]
        else:
            n = ys[aoff] * 4 + xs[boff]
        return pall.at[n, pl.ds(2 * chip[e] + rows[0], rows[1])]

    def send(e, sem, aoff, boff, rows, axis, step):
        ref = spot(e, aoff, boff, rows)
        to = beside[(lead(e) if axis == "a" else 1 - lead(e), step)]
        remote(ref, ref, ss, sem, to).start()

    def both(e, ident, aoff):
        send(e, rs.at[e, ident], aoff, 0, ALL, "b", 1)
        send(e, rs.at[e, ident + 1], aoff, 0, ALL, "b", -1)

    def first(e):
        if e == 0:
            take(pall.at[q, partner], zr.at[0])
        else:
            take(pall.at[q, pl.ds(2 * chip[e], 2)], zr.at[e])
        send(e, rs.at[e, 0], 0, 0, ALL, "a", 1)
        send(e, rs.at[e, 1], 0, 0, ALL, "a", -1)
        both(e, 4, 0)

    def second(e):
        take(spot(e, -1, 0, ALL), rs.at[e, 0])
        send(e, rs.at[e, 2], -1, 0, LO, "a", 1)
        both(e, 6, -1)
        take(spot(e, 1, 0, ALL), rs.at[e, 1])
        send(e, rs.at[e, 2], 1, 0, HI, "a", -1)
        both(e, 8, 1)

    def opposite(e):
        take(spot(e, 2, 0, ALL), rs.at[e, 2])
        both(e, 10, 2)

    def onward(e, aoff):
        i = ORDER[aoff]
        take(spot(e, aoff, -1, ALL), rs.at[e, 4 + 2 * i])
        send(e, rl_, aoff, -1, LO, "b", 1)
        take(spot(e, aoff, 1, ALL), rs.at[e, 5 + 2 * i])
        send(e, rl_, aoff, 1, HI, "b", -1)

    first(0)

    loads[1].wait()
    for kk in range(7):
        for t in range(32):
            af[kk, pl.ds(t, 4, stride=32), :] = araw[kk, :, t * 128 : t * 128 + 128].astype(jnp.float32)
    for kk in range(7):
        for r in range(4):
            amine[r, kk] = af[kk, 32 * r : 32 * r + 32, :].astype(jnp.bfloat16)
    loads[2].wait()
    none = jnp.full((4, 4), -1, jnp.int32)
    for h in (0, 1):
        pieces = []
        for kk in range(4 * h, 4 * h + 4):
            pieces += [sraw[kk], none] if kk < 7 else [jnp.full((4, 32), -1, jnp.int32)]
        imine[h] = jnp.concatenate(pieces, axis=1)
    loads[3].wait()

    def a_part(t):
        return abuf.at[t % 4, pl.ds((t // 4) * 4, 4)]

    a_own = abuf.at[layer, pl.ds(half * 4, 4)]
    own = [pltpu.make_async_copy(amine, a_own, ls.at[4]), pltpu.make_async_copy(imine, ibuf.at[part_of_j], ls.at[5])]
    for c in own:
        c.start()
    a_from = {e: 2 * chip[e] + core for e in (1, 2, 3)}
    for e in (2, 1, 3):
        remote(amine, a_own, as_.at[0], ar.at[e], in_column(2 * m4(z - e) + core)).start()
    remote(amine, a_own, as_.at[1], ar.at[0], in_column(partner)).start()
    for to in targets:
        remote(imine, ibuf.at[part_of_j], is_, ir, to).start()
        remote(cbuf.at[part_of_j], cbuf.at[part_of_j], cs, cr, to).start()

    def a_step(e):
        ref = a_part(a_from[e])
        take(ref, ar.at[e])
        remote(ref, ref, as_.at[1], ar.at[0], in_column(partner)).start()

    for e in QUARTERS[1:]:
        first(e)
    for l in range(4):
        base = l * 256 + 224
        prod_hi[base : base + 32, :] = jnp.zeros((32, 512), jnp.bfloat16)
        prod_lo[base : base + 32, :] = jnp.zeros((32, 512), jnp.bfloat16)
    for e in QUARTERS:
        second(e)
    for e in QUARTERS:
        onward(e, 0)
    take(ibuf.at[pl.ds(0, 7)], ir)
    take(cbuf.at[pl.ds(0, 7)], cr)
    for c in own:
        c.wait()
    cols = pltpu.make_async_copy(cbuf, csm, smem_sem)
    cols.start()

    target = lax.broadcasted_iota(jnp.int32, (128, 256), 0)

    def choose(r, carry):
        for l in range(4):
            s = [ibuf[l * 2 + r // 4, h, pl.ds(r % 4, 1)] for h in (0, 1)]
            lanes = jnp.concatenate(s, axis=1)
            oh[r, l] = jnp.where(lanes == target, 1.0, 0.0).astype(jnp.bfloat16)
        for n, e in enumerate(QUARTERS):
            pl.when(r == 2 * n)(lambda e=e: opposite(e))
        return carry

    lax.fori_loop(0, 8, choose, 0)
    for e in QUARTERS:
        onward(e, -1)
    a_step(1)
    a_step(3)
    a_step(2)
    take(abuf.at[pl.ds(0, 2)], ar.at[0])

    left = lax.broadcasted_iota(jnp.int32, (64, 128), 1) < 64

    def weigh(r, carry):
        for l in range(4):
            for kk in range(7):
                even_odd = abuf[l, r, kk]
                odd_even = jnp.concatenate([even_odd[:, 64:], even_odd[:, :64]], axis=1)
                zero = jnp.zeros((64, 128), jnp.bfloat16)
                wbuf[l, r, kk, 0:64] = jnp.where(left, jnp.concatenate([even_odd, odd_even], axis=0), zero)
                wbuf[l, r, kk, 64:128] = jnp.where(left, zero, jnp.concatenate([odd_even, even_odd], axis=0))
        for n, e in enumerate(QUARTERS):
            pl.when(r == n)(lambda e=e: onward(e, 1))
            pl.when(r == n + 4)(lambda e=e: onward(e, 2))
        return carry

    lax.fori_loop(0, 8, weigh, 0)
    cols.wait()
    take(pall.at[pl.ds(0, 4)], rl_)

    def row_product(r):
        rh, rl = r // 4, r % 4
        for l in range(4):
            for kk in range(7):
                col = csm[l * 2 + rh, rl, kk]
                prod = lax.dot_general(
                    pall[col // 8, col % 8], wbuf[l, r, kk], (((1,), (1,)), ((), ())),
                    preferred_element_type=jnp.float32,
                )
                moved = pltpu.roll(prod, ROWS - 4, 0)
                base = l * 256 + kk * 32
                for cp in range(4):
                    part = prod[28 * cp : 28 * cp + 32] if cp % 2 == 0 else moved[28 * cp - 4 : 28 * cp + 28]
                    hi = part.astype(jnp.bfloat16)
                    lo = (part - hi.astype(jnp.float32)).astype(jnp.bfloat16)
                    prod_hi[base : base + 32, cp * 128 : cp * 128 + 128] = hi
                    prod_lo[base : base + 32, cp * 128 : cp * 128 + 128] = lo
        total = jnp.zeros((128, 512), jnp.float32)
        for l in range(4):
            total += jnp.dot(oh[r, l], prod_hi[l * 256 : l * 256 + 256], preferred_element_type=jnp.float32)
            total += jnp.dot(oh[r, l], prod_lo[l * 256 : l * 256 + 256], preferred_element_type=jnp.float32)
        return total.astype(jnp.bfloat16)

    def one_row(n, carry):
        p = n // 2
        e = (2 + 2 * (p // 2) + (p // 2 + p) % 2) % 4
        r = 2 * ((z + e) % 4) + (core + 1 + n) % 2
        obuf[n] = row_product(r)

        @pl.when(n < 7)
        def _():
            remote(obuf.at[n], out.at[j], os, orr, in_column(r)).start()

        return carry

    lax.fori_loop(0, 8, one_row, 0)
    out[j] = obuf[7]

    take(pall.at[q, pl.ds(0, 7)], zs)
    take(abuf.at[pl.ds(0, 3), pl.ds(0, 4)], as_.at[0])
    take(abuf.at[pl.ds(0, 2)], as_.at[1])
    take(ibuf.at[pl.ds(0, 7)], is_)
    take(cbuf.at[pl.ds(0, 7)], cs)
    take(pall.at[pl.ds(0, 15)], ss)
    take(obuf.at[pl.ds(0, 7)], os)
    take(out.at[pl.ds(0, 7)], orr)


def per_device(a_blocks, a_cols, p_blocks, slots):
    dma = pltpu.SemaphoreType.DMA
    hbm = pl.BlockSpec(memory_space=pltpu.HBM)
    got = pl.pallas_call(
        kernel,
        out_shape=jax.ShapeDtypeStruct((8, 128, 512), jnp.bfloat16),
        in_specs=[hbm, hbm, hbm, hbm],
        out_specs=pl.BlockSpec(memory_space=pltpu.VMEM),
        scratch_shapes=[
            pltpu.VMEM((28, 4096), jnp.bfloat16),
            pltpu.VMEM((7, 4, 4096), jnp.bfloat16),
            pltpu.VMEM((7, 4, 28), jnp.int32),
            pltpu.VMEM((8, ROWS, 128), jnp.float32),
            pltpu.VMEM((8, ROWS, 128), jnp.bfloat16),
            pltpu.VMEM((7, 128, 128), jnp.float32),
            pltpu.VMEM((4, 7, 32, 128), jnp.bfloat16),
            pltpu.VMEM((2, 4, 128), jnp.int32),
            pltpu.VMEM((16, 8, ROWS, 128), jnp.bfloat16),
            pltpu.VMEM((4, 8, 7, 32, 128), jnp.bfloat16),
            pltpu.VMEM((8, 2, 4, 128), jnp.int32),
            pltpu.VMEM((8, 4, 7), jnp.int32),
            pltpu.SMEM((8, 4, 7), jnp.int32),
            pltpu.VMEM((4, 8, 7, 128, 128), jnp.bfloat16),
            pltpu.VMEM((8, 4, 128, 256), jnp.bfloat16),
            pltpu.VMEM((1024, 512), jnp.bfloat16),
            pltpu.VMEM((1024, 512), jnp.bfloat16),
            pltpu.VMEM((8, 128, 512), jnp.bfloat16),
            dma((6,)), dma, dma((4,)), dma((2,)), dma((4,)), dma, dma, dma, dma,
            dma, dma((4, 12)), dma, dma, dma, dma,
        ],
        compiler_params=pltpu.CompilerParams(
            collective_id=0, has_side_effects=True, vmem_limit_bytes=60 * 2**20
        ),
        name="column_split",
    )(p_blocks[0], a_blocks.transpose(1, 0, 2), slots.transpose(1, 0, 2), a_cols)
    got = got.reshape(8, 128, 4, 2, 2, 32).transpose(1, 5, 4, 0, 2, 3)
    return got.reshape(1, 128, 4096)


def solution(mesh):
    placed = (
        P("grid", "layer", None),
        P("grid", "layer"),
        P(("grid", "layer"), None, None),
        P("grid", "layer", None),
    )
    return jax.shard_map(
        per_device,
        mesh=mesh,
        in_specs=placed,
        out_specs=P(("grid", "layer"), None, None),
        check_vma=False,
    )
```

```python
import jax
import jax.numpy as jnp
from jax import lax
from jax.experimental import pallas as pl
from jax.experimental.pallas import tpu as pltpu
from jax.sharding import PartitionSpec as P

MESH = pl.DeviceIdType.MESH
ROWS = 112
ALL, LO, HI = (0, 2), (0, 1), (1, 1)
ORDER = {0: 0, -1: 1, 1: 2, 2: 3}
QUARTERS = (0, 1, 3, 2)


def place():
    g, l = lax.axis_index("grid"), lax.axis_index("layer")
    return g // 8, (g // 2) % 4, (g % 2) * 4 + l


def dev(y, x, j):
    return ((y * 4 + x) * 2 + j // 4, j % 4)


def m4(v):
    return lax.rem(v + 4, 4)


def columns_out(tiles):
    lane = lax.broadcasted_iota(jnp.int32, tiles[0].shape, 1)
    for i in range(5):
        d, up = 2 << i, (lane & (2 << i)) != 0
        swapped = list(tiles)
        for t in range(32):
            if not t & (1 << i):
                low, high = tiles[t], tiles[t | (1 << i)]
                swapped[t] = jnp.where(up, pltpu.roll(high, d, 1), low)
                swapped[t | (1 << i)] = jnp.where(up, high, pltpu.roll(low, 128 - d, 1))
        tiles = swapped
    top, bottom = (lane & 64) != 0, (lane & 1) != 0
    done = []
    for v in tiles:
        moved = jnp.where(top, pltpu.roll(v, 63, 1), pltpu.roll(v, 65, 1))
        done.append(jnp.where(top == bottom, v, moved))
    return done


def kernel(
    p_raw, a_raw, slot_raw, col_src, out,
    praw, araw, sraw, pf, pt, af, amine, imine,
    pall, abuf, ibuf, cbuf, csm, wbuf, oh, prod_hi, prod_lo, of, obuf,
    ls, zs, zr, as_, ar, is_, ir, cs, cr, ss, rs, rl_, os, orr, smem_sem,
):
    y, x, j = place()
    q, z, core = y * 4 + x, j // 2, j % 2
    half, layer = j // 4, j % 4
    part_of_j = layer * 2 + half
    partner = j + 1 - 2 * core
    xs = {0: x, 1: m4(x + 1), 2: m4(x + 2), -1: m4(x - 1)}
    ys = {0: y, 1: m4(y + 1), 2: m4(y + 2), -1: m4(y - 1)}
    beside = {(0, 1): dev(y, xs[1], j), (0, -1): dev(y, xs[-1], j), (1, 1): dev(ys[1], x, j), (1, -1): dev(ys[-1], x, j)}
    chip = {e: m4(z + e) for e in range(4)}

    def in_column(t):
        return (q * 2 + t // 4, t % 4)

    targets = [in_column(lax.rem(j + d, 8)) for d in range(1, 8)]
    barrier = pltpu.get_barrier_semaphore()
    for to in targets + list(beside.values()):
        pl.semaphore_signal(barrier, inc=1, device_id=to, device_id_type=MESH)
    loads = [
        pltpu.make_async_copy(p_raw, praw, ls.at[0]),
        pltpu.make_async_copy(a_raw, araw, ls.at[1]),
        pltpu.make_async_copy(slot_raw, sraw, ls.at[2]),
        pltpu.make_async_copy(col_src, cbuf.at[part_of_j], ls.at[3]),
    ]
    for c in loads:
        c.start()

    def remote(s, d, ssem, rsem, to):
        return pltpu.make_async_remote_copy(
            src_ref=s, dst_ref=d, send_sem=ssem, recv_sem=rsem, device_id=to, device_id_type=MESH
        )

    def take(ref, sem):
        pltpu.make_async_copy(ref, ref, sem).wait()

    loads[0].wait()
    for m in (0, 8, 16, 24):
        rows = min(8, 28 - m)
        tiles = []
        for t in range(32):
            v = praw[m : m + rows, t * 128 : t * 128 + 128].astype(jnp.float32)
            tiles.append(v if rows == 8 else jnp.concatenate([v, v], axis=0))
        for t, v in enumerate(columns_out(tiles)):
            at = (t % 4) * 28 + m
            pf[t // 4, at : at + rows, :] = v[:rows]
    for t in range(8):
        pt[t] = pf[t].astype(jnp.bfloat16)
    pall[q, j] = pt[j]
    pl.semaphore_wait(barrier, 11)

    remote(pt.at[partner], pall.at[q, j], zs, zr.at[0], in_column(partner)).start()
    for e in (1, 3, 2):
        for c in (0, 1):
            t = 2 * m4(z - e) + c
            remote(pt.at[t], pall.at[q, j], zs, zr.at[e], in_column(t)).start()

    def lead(e):
        return 0 if e in (0, 3) else 1

    def spot(e, aoff, boff, rows):
        if lead(e) == 0:
            n = ys[boff] * 4 + xs[aoff]
        else:
            n = ys[aoff] * 4 + xs[boff]
        return pall.at[n, pl.ds(2 * chip[e] + rows[0], rows[1])]

    def send(e, sem, aoff, boff, rows, axis, step):
        ref = spot(e, aoff, boff, rows)
        to = beside[(lead(e) if axis == "a" else 1 - lead(e), step)]
        remote(ref, ref, ss, sem, to).start()

    def both(e, ident, aoff):
        send(e, rs.at[e, ident], aoff, 0, ALL, "b", 1)
        send(e, rs.at[e, ident + 1], aoff, 0, ALL, "b", -1)

    def first(e):
        if e == 0:
            take(pall.at[q, partner], zr.at[0])
        else:
            take(pall.at[q, pl.ds(2 * chip[e], 2)], zr.at[e])
        send(e, rs.at[e, 0], 0, 0, ALL, "a", 1)
        send(e, rs.at[e, 1], 0, 0, ALL, "a", -1)
        both(e, 4, 0)

    def second(e):
        take(spot(e, -1, 0, ALL), rs.at[e, 0])
        send(e, rs.at[e, 2], -1, 0, LO, "a", 1)
        both(e, 6, -1)
        take(spot(e, 1, 0, ALL), rs.at[e, 1])
        send(e, rs.at[e, 2], 1, 0, HI, "a", -1)
        both(e, 8, 1)

    def opposite(e):
        take(spot(e, 2, 0, ALL), rs.at[e, 2])
        both(e, 10, 2)

    def onward(e, aoff):
        i = ORDER[aoff]
        take(spot(e, aoff, -1, ALL), rs.at[e, 4 + 2 * i])
        send(e, rl_, aoff, -1, LO, "b", 1)
        take(spot(e, aoff, 1, ALL), rs.at[e, 5 + 2 * i])
        send(e, rl_, aoff, 1, HI, "b", -1)

    first(0)

    loads[1].wait()
    for kk in range(7):
        for t in range(32):
            af[kk, pl.ds(t, 4, stride=32), :] = araw[kk, :, t * 128 : t * 128 + 128].astype(jnp.float32)
    for kk in range(7):
        for r in range(4):
            amine[r, kk] = af[kk, 32 * r : 32 * r + 32, :].astype(jnp.bfloat16)
    loads[2].wait()
    none = jnp.full((4, 4), -1, jnp.int32)
    for h in (0, 1):
        pieces = []
        for kk in range(4 * h, 4 * h + 4):
            pieces += [sraw[kk], none] if kk < 7 else [jnp.full((4, 32), -1, jnp.int32)]
        imine[h] = jnp.concatenate(pieces, axis=1)
    loads[3].wait()

    def a_part(t):
        return abuf.at[t % 4, pl.ds((t // 4) * 4, 4)]

    a_own = abuf.at[layer, pl.ds(half * 4, 4)]
    own = [pltpu.make_async_copy(amine, a_own, ls.at[4]), pltpu.make_async_copy(imine, ibuf.at[part_of_j], ls.at[5])]
    for c in own:
        c.start()
    a_from = {e: 2 * chip[e] + core for e in (1, 2, 3)}
    for e in (2, 1, 3):
        remote(amine, a_own, as_.at[0], ar.at[e], in_column(2 * m4(z - e) + core)).start()
    remote(amine, a_own, as_.at[1], ar.at[0], in_column(partner)).start()
    for to in targets:
        remote(imine, ibuf.at[part_of_j], is_, ir, to).start()
        remote(cbuf.at[part_of_j], cbuf.at[part_of_j], cs, cr, to).start()

    def a_step(e):
        ref = a_part(a_from[e])
        take(ref, ar.at[e])
        remote(ref, ref, as_.at[1], ar.at[0], in_column(partner)).start()

    for e in QUARTERS[1:]:
        first(e)
    for l in range(4):
        base = l * 256 + 224
        prod_hi[base : base + 32, :] = jnp.zeros((32, 512), jnp.bfloat16)
        prod_lo[base : base + 32, :] = jnp.zeros((32, 512), jnp.bfloat16)
    for e in QUARTERS:
        second(e)
    for e in QUARTERS:
        onward(e, 0)
    take(ibuf.at[pl.ds(0, 7)], ir)
    take(cbuf.at[pl.ds(0, 7)], cr)
    for c in own:
        c.wait()
    cols = pltpu.make_async_copy(cbuf, csm, smem_sem)
    cols.start()

    target = lax.broadcasted_iota(jnp.int32, (128, 256), 0)

    def choose(r, carry):
        for l in range(4):
            s = [ibuf[l * 2 + r // 4, h, pl.ds(r % 4, 1)] for h in (0, 1)]
            lanes = jnp.concatenate(s, axis=1)
            oh[r, l] = jnp.where(lanes == target, 1.0, 0.0).astype(jnp.bfloat16)
        for n, e in enumerate(QUARTERS):
            pl.when(r == 2 * n)(lambda e=e: opposite(e))
        return carry

    lax.fori_loop(0, 8, choose, 0)
    for e in QUARTERS:
        onward(e, -1)
    a_step(1)
    a_step(3)
    a_step(2)
    take(abuf.at[pl.ds(0, 2)], ar.at[0])

    left = lax.broadcasted_iota(jnp.int32, (64, 128), 1) < 64

    def weigh(r, carry):
        for l in range(4):
            for kk in range(7):
                even_odd = abuf[l, r, kk]
                odd_even = jnp.concatenate([even_odd[:, 64:], even_odd[:, :64]], axis=1)
                zero = jnp.zeros((64, 128), jnp.bfloat16)
                wbuf[l, r, kk, 0:64] = jnp.where(left, jnp.concatenate([even_odd, odd_even], axis=0), zero)
                wbuf[l, r, kk, 64:128] = jnp.where(left, zero, jnp.concatenate([odd_even, even_odd], axis=0))
        for n, e in enumerate(QUARTERS):
            pl.when(r == n)(lambda e=e: onward(e, 1))
            pl.when(r == n + 4)(lambda e=e: onward(e, 2))
        return carry

    lax.fori_loop(0, 8, weigh, 0)
    cols.wait()
    take(pall.at[pl.ds(0, 4)], rl_)

    def row_product(r):
        rh, rl = r // 4, r % 4
        for l in range(4):
            for kk in range(7):
                col = csm[l * 2 + rh, rl, kk]
                prod = lax.dot_general(
                    pall[col // 8, col % 8], wbuf[l, r, kk], (((1,), (1,)), ((), ())),
                    preferred_element_type=jnp.float32,
                )
                moved = pltpu.roll(prod, ROWS - 4, 0)
                base = l * 256 + kk * 32
                for cp in range(4):
                    part = prod[28 * cp : 28 * cp + 32] if cp % 2 == 0 else moved[28 * cp - 4 : 28 * cp + 28]
                    hi = part.astype(jnp.bfloat16)
                    lo = (part - hi.astype(jnp.float32)).astype(jnp.bfloat16)
                    prod_hi[base : base + 32, cp * 128 : cp * 128 + 128] = hi
                    prod_lo[base : base + 32, cp * 128 : cp * 128 + 128] = lo
        total = jnp.zeros((128, 512), jnp.float32)
        for l in range(4):
            total += jnp.dot(oh[r, l], prod_hi[l * 256 : l * 256 + 256], preferred_element_type=jnp.float32)
            total += jnp.dot(oh[r, l], prod_lo[l * 256 : l * 256 + 256], preferred_element_type=jnp.float32)
        for cp in range(4):
            turned = total[:, cp * 128 : cp * 128 + 128].T
            for c0 in (0, 1):
                for a0 in (0, 1):
                    n = 64 * c0 + 32 * a0
                    of[pl.ds(8 * a0 + 2 * cp + c0, 32, stride=16), :] = turned[n : n + 32]
        return of[...].reshape(64, 8, 128).astype(jnp.bfloat16)

    def one_row(n, carry):
        p = n // 2
        e = (2 + 2 * (p // 2) + (p // 2 + p) % 2) % 4
        r = 2 * ((z + e) % 4) + (core + 1 + n) % 2
        obuf[n] = row_product(r)

        @pl.when(n < 7)
        def _():
            remote(obuf.at[n], out.at[:, j], os, orr, in_column(r)).start()

        return carry

    lax.fori_loop(0, 8, one_row, 0)
    out[:, j] = obuf[7]

    take(pall.at[q, pl.ds(0, 7)], zs)
    take(abuf.at[pl.ds(0, 3), pl.ds(0, 4)], as_.at[0])
    take(abuf.at[pl.ds(0, 2)], as_.at[1])
    take(ibuf.at[pl.ds(0, 7)], is_)
    take(cbuf.at[pl.ds(0, 7)], cs)
    take(pall.at[pl.ds(0, 15)], ss)
    take(obuf.at[pl.ds(0, 7)], os)
    take(out.at[:, pl.ds(0, 7)], orr)


def per_device(a_blocks, a_cols, p_blocks, slots):
    dma = pltpu.SemaphoreType.DMA
    hbm = pl.BlockSpec(memory_space=pltpu.HBM)
    got = pl.pallas_call(
        kernel,
        out_shape=jax.ShapeDtypeStruct((64, 8, 8, 128), jnp.bfloat16),
        in_specs=[hbm, hbm, hbm, hbm],
        out_specs=pl.BlockSpec(memory_space=pltpu.VMEM),
        scratch_shapes=[
            pltpu.VMEM((28, 4096), jnp.bfloat16),
            pltpu.VMEM((7, 4, 4096), jnp.bfloat16),
            pltpu.VMEM((7, 4, 28), jnp.int32),
            pltpu.VMEM((8, ROWS, 128), jnp.float32),
            pltpu.VMEM((8, ROWS, 128), jnp.bfloat16),
            pltpu.VMEM((7, 128, 128), jnp.float32),
            pltpu.VMEM((4, 7, 32, 128), jnp.bfloat16),
            pltpu.VMEM((2, 4, 128), jnp.int32),
            pltpu.VMEM((16, 8, ROWS, 128), jnp.bfloat16),
            pltpu.VMEM((4, 8, 7, 32, 128), jnp.bfloat16),
            pltpu.VMEM((8, 2, 4, 128), jnp.int32),
            pltpu.VMEM((8, 4, 7), jnp.int32),
            pltpu.SMEM((8, 4, 7), jnp.int32),
            pltpu.VMEM((4, 8, 7, 128, 128), jnp.bfloat16),
            pltpu.VMEM((8, 4, 128, 256), jnp.bfloat16),
            pltpu.VMEM((1024, 512), jnp.bfloat16),
            pltpu.VMEM((1024, 512), jnp.bfloat16),
            pltpu.VMEM((512, 128), jnp.float32),
            pltpu.VMEM((8, 64, 8, 128), jnp.bfloat16),
            dma((6,)), dma, dma((4,)), dma((2,)), dma((4,)), dma, dma, dma, dma,
            dma, dma((4, 12)), dma, dma, dma, dma,
        ],
        compiler_params=pltpu.CompilerParams(
            collective_id=0, has_side_effects=True, vmem_limit_bytes=60 * 2**20
        ),
        name="column_split",
    )(p_blocks[0], a_blocks.transpose(1, 0, 2), slots.transpose(1, 0, 2), a_cols)
    return got.reshape(4096, 128).T[None]


def solution(mesh):
    placed = (
        P("grid", "layer", None),
        P("grid", "layer"),
        P(("grid", "layer"), None, None),
        P("grid", "layer", None),
    )
    return jax.shard_map(
        per_device,
        mesh=mesh,
        in_specs=placed,
        out_specs=P(("grid", "layer"), None, None),
        check_vma=False,
    )
```

```python
import jax
import jax.numpy as jnp
from jax import lax
from jax.experimental import pallas as pl
from jax.experimental.pallas import tpu as pltpu
from jax.sharding import PartitionSpec as P

MESH = pl.DeviceIdType.MESH
ROWS = 112
ALL, LO, HI = (0, 2), (0, 1), (1, 1)
ORDER = {0: 0, -1: 1, 1: 2, 2: 3}
QUARTERS = (0, 1, 3, 2)


def place():
    g, l = lax.axis_index("grid"), lax.axis_index("layer")
    return g // 8, (g // 2) % 4, (g % 2) * 4 + l


def dev(y, x, j):
    return ((y * 4 + x) * 2 + j // 4, j % 4)


def m4(v):
    return lax.rem(v + 4, 4)


def columns_out(tiles):
    lane = lax.broadcasted_iota(jnp.int32, tiles[0].shape, 1)
    for i in range(5):
        d, up = 2 << i, (lane & (2 << i)) != 0
        swapped = list(tiles)
        for t in range(32):
            if not t & (1 << i):
                low, high = tiles[t], tiles[t | (1 << i)]
                swapped[t] = jnp.where(up, pltpu.roll(high, d, 1), low)
                swapped[t | (1 << i)] = jnp.where(up, high, pltpu.roll(low, 128 - d, 1))
        tiles = swapped
    top, bottom = (lane & 64) != 0, (lane & 1) != 0
    done = []
    for v in tiles:
        moved = jnp.where(top, pltpu.roll(v, 63, 1), pltpu.roll(v, 65, 1))
        done.append(jnp.where(top == bottom, v, moved))
    return done


def kernel(
    p_raw, a_raw, slot_raw, col_src, out,
    praw, araw, sraw, craw, pf, pt, af, amine, imine,
    pall, abuf, ibuf, csm, wbuf, oh, prod_hi, prod_lo, of, obuf,
    ls, zs, zr, as_, ar, is_, ir, ss, rs, rl_, os, orr, smem_sem,
):
    y, x, j = place()
    q, z, core = y * 4 + x, j // 2, j % 2
    half, layer = j // 4, j % 4
    part_of_j = layer * 2 + half
    partner = j + 1 - 2 * core
    xs = {0: x, 1: m4(x + 1), 2: m4(x + 2), -1: m4(x - 1)}
    ys = {0: y, 1: m4(y + 1), 2: m4(y + 2), -1: m4(y - 1)}
    beside = {(0, 1): dev(y, xs[1], j), (0, -1): dev(y, xs[-1], j), (1, 1): dev(ys[1], x, j), (1, -1): dev(ys[-1], x, j)}
    chip = {e: m4(z + e) for e in range(4)}

    def in_column(t):
        return (q * 2 + t // 4, t % 4)

    targets = [in_column(lax.rem(j + d, 8)) for d in range(1, 8)]
    barrier = pltpu.get_barrier_semaphore()
    for to in targets + list(beside.values()):
        pl.semaphore_signal(barrier, inc=1, device_id=to, device_id_type=MESH)
    loads = [
        pltpu.make_async_copy(p_raw, praw, ls.at[0]),
        pltpu.make_async_copy(a_raw, araw, ls.at[1]),
        pltpu.make_async_copy(slot_raw, sraw, ls.at[2]),
        pltpu.make_async_copy(col_src, craw, ls.at[3]),
    ]
    for c in loads:
        c.start()

    def remote(s, d, ssem, rsem, to):
        return pltpu.make_async_remote_copy(
            src_ref=s, dst_ref=d, send_sem=ssem, recv_sem=rsem, device_id=to, device_id_type=MESH
        )

    def take(ref, sem):
        pltpu.make_async_copy(ref, ref, sem).wait()

    loads[0].wait()
    for m in (0, 8, 16, 24):
        rows = min(8, 28 - m)
        tiles = []
        for t in range(32):
            v = praw[m : m + rows, t * 128 : t * 128 + 128].astype(jnp.float32)
            tiles.append(v if rows == 8 else jnp.concatenate([v, v], axis=0))
        for t, v in enumerate(columns_out(tiles)):
            at = (t % 4) * 28 + m
            pf[t // 4, at : at + rows, :] = v[:rows]
    for t in range(8):
        pt[t] = pf[t].astype(jnp.bfloat16)
    pall[q, j] = pt[j]
    pl.semaphore_wait(barrier, 11)

    remote(pt.at[partner], pall.at[q, j], zs, zr.at[0], in_column(partner)).start()
    for e in (1, 3, 2):
        for c in (0, 1):
            t = 2 * m4(z - e) + c
            remote(pt.at[t], pall.at[q, j], zs, zr.at[e], in_column(t)).start()

    def lead(e):
        return 0 if e in (0, 3) else 1

    def spot(e, aoff, boff, rows):
        if lead(e) == 0:
            n = ys[boff] * 4 + xs[aoff]
        else:
            n = ys[aoff] * 4 + xs[boff]
        return pall.at[n, pl.ds(2 * chip[e] + rows[0], rows[1])]

    def send(e, sem, aoff, boff, rows, axis, step):
        ref = spot(e, aoff, boff, rows)
        to = beside[(lead(e) if axis == "a" else 1 - lead(e), step)]
        remote(ref, ref, ss, sem, to).start()

    def both(e, ident, aoff):
        send(e, rs.at[e, ident], aoff, 0, ALL, "b", 1)
        send(e, rs.at[e, ident + 1], aoff, 0, ALL, "b", -1)

    def first(e):
        if e == 0:
            take(pall.at[q, partner], zr.at[0])
        else:
            take(pall.at[q, pl.ds(2 * chip[e], 2)], zr.at[e])
        send(e, rs.at[e, 0], 0, 0, ALL, "a", 1)
        send(e, rs.at[e, 1], 0, 0, ALL, "a", -1)
        both(e, 4, 0)

    def second(e):
        take(spot(e, -1, 0, ALL), rs.at[e, 0])
        send(e, rs.at[e, 2], -1, 0, LO, "a", 1)
        both(e, 6, -1)
        take(spot(e, 1, 0, ALL), rs.at[e, 1])
        send(e, rs.at[e, 2], 1, 0, HI, "a", -1)
        both(e, 8, 1)

    def opposite(e):
        take(spot(e, 2, 0, ALL), rs.at[e, 2])
        both(e, 10, 2)

    def onward(e, aoff):
        i = ORDER[aoff]
        take(spot(e, aoff, -1, ALL), rs.at[e, 4 + 2 * i])
        send(e, rl_, aoff, -1, LO, "b", 1)
        take(spot(e, aoff, 1, ALL), rs.at[e, 5 + 2 * i])
        send(e, rl_, aoff, 1, HI, "b", -1)

    first(0)

    loads[1].wait()
    for kk in range(7):
        for t in range(32):
            af[kk, pl.ds(t, 4, stride=32), :] = araw[kk, :, t * 128 : t * 128 + 128].astype(jnp.float32)
    for kk in range(7):
        for r in range(4):
            amine[r, kk] = af[kk, 32 * r : 32 * r + 32, :].astype(jnp.bfloat16)
    loads[2].wait()
    loads[3].wait()
    none = jnp.full((4, 4), -1, jnp.int32)
    for h in (0, 1):
        pieces = []
        for kk in range(4 * h, 4 * h + 4):
            pieces += [sraw[kk], none] if kk < 7 else [craw[...], jnp.full((4, 25), -1, jnp.int32)]
        imine[h] = jnp.concatenate(pieces, axis=1)

    def a_part(t):
        return abuf.at[t % 4, pl.ds((t // 4) * 4, 4)]

    a_own = abuf.at[layer, pl.ds(half * 4, 4)]
    own = [pltpu.make_async_copy(amine, a_own, ls.at[4]), pltpu.make_async_copy(imine, ibuf.at[part_of_j], ls.at[5])]
    for c in own:
        c.start()
    a_from = {e: 2 * chip[e] + core for e in (1, 2, 3)}
    for e in (2, 1, 3):
        remote(amine, a_own, as_.at[0], ar.at[e], in_column(2 * m4(z - e) + core)).start()
    remote(amine, a_own, as_.at[1], ar.at[0], in_column(partner)).start()
    for to in targets:
        remote(imine, ibuf.at[part_of_j], is_, ir, to).start()

    def a_step(e):
        ref = a_part(a_from[e])
        take(ref, ar.at[e])
        remote(ref, ref, as_.at[1], ar.at[0], in_column(partner)).start()

    for e in QUARTERS[1:]:
        first(e)
    for l in range(4):
        base = l * 256 + 224
        prod_hi[base : base + 32, :] = jnp.zeros((32, 512), jnp.bfloat16)
        prod_lo[base : base + 32, :] = jnp.zeros((32, 512), jnp.bfloat16)
    for e in QUARTERS:
        second(e)
    for e in QUARTERS:
        onward(e, 0)
    take(ibuf.at[pl.ds(0, 7)], ir)
    for c in own:
        c.wait()
    cols = pltpu.make_async_copy(ibuf.at[:, 1], csm, smem_sem)
    cols.start()

    target = lax.broadcasted_iota(jnp.int32, (128, 256), 0)

    def choose(r, carry):
        for l in range(4):
            s = [ibuf[l * 2 + r // 4, h, pl.ds(r % 4, 1)] for h in (0, 1)]
            lanes = jnp.concatenate(s, axis=1)
            oh[r, l] = jnp.where(lanes == target, 1.0, 0.0).astype(jnp.bfloat16)
        for n, e in enumerate(QUARTERS):
            pl.when(r == 2 * n)(lambda e=e: opposite(e))
        return carry

    lax.fori_loop(0, 8, choose, 0)
    for e in QUARTERS:
        onward(e, -1)
    for e in QUARTERS:
        onward(e, 1)
    a_step(1)
    a_step(3)
    a_step(2)
    for e in QUARTERS:
        onward(e, 2)

    left = lax.broadcasted_iota(jnp.int32, (64, 128), 1) < 64

    def weigh(r):
        for l in range(4):
            for kk in range(7):
                even_odd = abuf[l, r, kk]
                odd_even = jnp.concatenate([even_odd[:, 64:], even_odd[:, :64]], axis=1)
                zero = jnp.zeros((64, 128), jnp.bfloat16)
                wbuf[l, kk, 0:64] = jnp.where(left, jnp.concatenate([even_odd, odd_even], axis=0), zero)
                wbuf[l, kk, 64:128] = jnp.where(left, zero, jnp.concatenate([odd_even, even_odd], axis=0))

    cols.wait()

    def row_product(r):
        rh, rl = r // 4, r % 4
        for l in range(4):
            for kk in range(7):
                col = csm[l * 2 + rh, rl, 96 + kk]
                prod = lax.dot_general(
                    pall[col // 8, col % 8], wbuf[l, kk], (((1,), (1,)), ((), ())),
                    preferred_element_type=jnp.float32,
                )
                moved = pltpu.roll(prod, ROWS - 4, 0)
                base = l * 256 + kk * 32
                for cp in range(4):
                    part = prod[28 * cp : 28 * cp + 32] if cp % 2 == 0 else moved[28 * cp - 4 : 28 * cp + 28]
                    hi = part.astype(jnp.bfloat16)
                    lo = (part - hi.astype(jnp.float32)).astype(jnp.bfloat16)
                    prod_hi[base : base + 32, cp * 128 : cp * 128 + 128] = hi
                    prod_lo[base : base + 32, cp * 128 : cp * 128 + 128] = lo
        total = jnp.zeros((128, 512), jnp.float32)
        for l in range(4):
            total += jnp.dot(oh[r, l], prod_hi[l * 256 : l * 256 + 256], preferred_element_type=jnp.float32)
            total += jnp.dot(oh[r, l], prod_lo[l * 256 : l * 256 + 256], preferred_element_type=jnp.float32)
        for cp in range(4):
            turned = total[:, cp * 128 : cp * 128 + 128].T
            for c0 in (0, 1):
                for a0 in (0, 1):
                    n = 64 * c0 + 32 * a0
                    of[pl.ds(8 * a0 + 2 * cp + c0, 32, stride=16), :] = turned[n : n + 32]
        return of[...].reshape(64, 8, 128).astype(jnp.bfloat16)

    def turn(n):
        p = n // 2
        e = (2 + 2 * (p // 2) + (p // 2 + p) % 2) % 4
        return 2 * ((z + e) % 4) + (core + 1 + n) % 2

    def one_row(n, carry):
        r = turn(n)
        obuf[n] = row_product(r)

        @pl.when(n < 7)
        def _():
            remote(obuf.at[n], out.at[:, j], os, orr, in_column(r)).start()
            weigh(turn(n + 1))

        return carry

    take(abuf.at[pl.ds(0, 2)], ar.at[0])
    weigh(turn(0))
    take(pall.at[pl.ds(0, 4)], rl_)
    lax.fori_loop(0, 8, one_row, 0)
    out[:, j] = obuf[7]

    take(pall.at[q, pl.ds(0, 7)], zs)
    take(abuf.at[pl.ds(0, 3), pl.ds(0, 4)], as_.at[0])
    take(abuf.at[pl.ds(0, 2)], as_.at[1])
    take(ibuf.at[pl.ds(0, 7)], is_)
    take(pall.at[pl.ds(0, 15)], ss)
    take(obuf.at[pl.ds(0, 7)], os)
    take(out.at[:, pl.ds(0, 7)], orr)


def per_device(a_blocks, a_cols, p_blocks, slots):
    dma = pltpu.SemaphoreType.DMA
    hbm = pl.BlockSpec(memory_space=pltpu.HBM)
    got = pl.pallas_call(
        kernel,
        out_shape=jax.ShapeDtypeStruct((64, 8, 8, 128), jnp.bfloat16),
        in_specs=[hbm, hbm, hbm, hbm],
        out_specs=pl.BlockSpec(memory_space=pltpu.VMEM),
        scratch_shapes=[
            pltpu.VMEM((28, 4096), jnp.bfloat16),
            pltpu.VMEM((7, 4, 4096), jnp.bfloat16),
            pltpu.VMEM((7, 4, 28), jnp.int32),
            pltpu.VMEM((4, 7), jnp.int32),
            pltpu.VMEM((8, ROWS, 128), jnp.float32),
            pltpu.VMEM((8, ROWS, 128), jnp.bfloat16),
            pltpu.VMEM((7, 128, 128), jnp.float32),
            pltpu.VMEM((4, 7, 32, 128), jnp.bfloat16),
            pltpu.VMEM((2, 4, 128), jnp.int32),
            pltpu.VMEM((16, 8, ROWS, 128), jnp.bfloat16),
            pltpu.VMEM((4, 8, 7, 32, 128), jnp.bfloat16),
            pltpu.VMEM((8, 2, 4, 128), jnp.int32),
            pltpu.SMEM((8, 4, 128), jnp.int32),
            pltpu.VMEM((4, 7, 128, 128), jnp.bfloat16),
            pltpu.VMEM((8, 4, 128, 256), jnp.bfloat16),
            pltpu.VMEM((1024, 512), jnp.bfloat16),
            pltpu.VMEM((1024, 512), jnp.bfloat16),
            pltpu.VMEM((512, 128), jnp.float32),
            pltpu.VMEM((8, 64, 8, 128), jnp.bfloat16),
            dma((6,)), dma, dma((4,)), dma((2,)), dma((4,)), dma, dma,
            dma, dma((4, 12)), dma, dma, dma, dma,
        ],
        compiler_params=pltpu.CompilerParams(
            collective_id=0, has_side_effects=True, vmem_limit_bytes=60 * 2**20
        ),
        name="column_split",
    )(p_blocks[0], a_blocks.transpose(1, 0, 2), slots.transpose(1, 0, 2), a_cols)
    return got.reshape(4096, 128).T[None]


def solution(mesh):
    placed = (
        P("grid", "layer", None),
        P("grid", "layer"),
        P(("grid", "layer"), None, None),
        P("grid", "layer", None),
    )
    return jax.shard_map(
        per_device,
        mesh=mesh,
        in_specs=placed,
        out_specs=P(("grid", "layer"), None, None),
        check_vma=False,
    )
```

```python
import jax
import jax.numpy as jnp
from jax import lax
from jax.experimental import pallas as pl
from jax.experimental.pallas import tpu as pltpu
from jax.sharding import PartitionSpec as P

MESH = pl.DeviceIdType.MESH
ROWS = 112
ALL, LO, HI = (0, 2), (0, 1), (1, 1)
ORDER = {0: 0, -1: 1, 1: 2, 2: 3}
QUARTERS = (0, 1, 3, 2)


def place():
    g, l = lax.axis_index("grid"), lax.axis_index("layer")
    return g // 8, (g // 2) % 4, (g % 2) * 4 + l


def dev(y, x, j):
    return ((y * 4 + x) * 2 + j // 4, j % 4)


def m4(v):
    return lax.rem(v + 4, 4)


def columns_out(tiles):
    lane = lax.broadcasted_iota(jnp.int32, tiles[0].shape, 1)
    for i in range(5):
        d, up = 2 << i, (lane & (2 << i)) != 0
        swapped = list(tiles)
        for t in range(32):
            if not t & (1 << i):
                low, high = tiles[t], tiles[t | (1 << i)]
                swapped[t] = jnp.where(up, pltpu.roll(high, d, 1), low)
                swapped[t | (1 << i)] = jnp.where(up, high, pltpu.roll(low, 128 - d, 1))
        tiles = swapped
    top, bottom = (lane & 64) != 0, (lane & 1) != 0
    done = []
    for v in tiles:
        moved = jnp.where(top, pltpu.roll(v, 63, 1), pltpu.roll(v, 65, 1))
        done.append(jnp.where(top == bottom, v, moved))
    return done


def kernel(
    p_raw, a_raw, slot_raw, col_src, out,
    praw, araw, sraw, craw, pf, pt, af, amine, imine,
    pall, abuf, ibuf, csm, wbuf, oh, prod_hi, prod_lo, of, obuf,
    ls, zs, zr, as_, ar, is_, ir, ss, rs, rl_, os, orr, smem_sem,
):
    y, x, j = place()
    q, z, core = y * 4 + x, j // 2, j % 2
    half, layer = j // 4, j % 4
    part_of_j = layer * 2 + half
    partner = j + 1 - 2 * core
    xs = {0: x, 1: m4(x + 1), 2: m4(x + 2), -1: m4(x - 1)}
    ys = {0: y, 1: m4(y + 1), 2: m4(y + 2), -1: m4(y - 1)}
    beside = {(0, 1): dev(y, xs[1], j), (0, -1): dev(y, xs[-1], j), (1, 1): dev(ys[1], x, j), (1, -1): dev(ys[-1], x, j)}
    chip = {e: m4(z + e) for e in range(4)}

    def in_column(t):
        return (q * 2 + t // 4, t % 4)

    targets = [in_column(lax.rem(j + d, 8)) for d in range(1, 8)]
    barrier = pltpu.get_barrier_semaphore()
    for to in targets + list(beside.values()):
        pl.semaphore_signal(barrier, inc=1, device_id=to, device_id_type=MESH)
    loads = [
        pltpu.make_async_copy(p_raw, praw, ls.at[0]),
        pltpu.make_async_copy(a_raw, araw, ls.at[1]),
        pltpu.make_async_copy(slot_raw, sraw, ls.at[2]),
        pltpu.make_async_copy(col_src, craw, ls.at[3]),
    ]
    for c in loads:
        c.start()

    def remote(s, d, ssem, rsem, to):
        return pltpu.make_async_remote_copy(
            src_ref=s, dst_ref=d, send_sem=ssem, recv_sem=rsem, device_id=to, device_id_type=MESH
        )

    def take(ref, sem):
        pltpu.make_async_copy(ref, ref, sem).wait()

    loads[0].wait()
    for m in (0, 8, 16, 24):
        rows = min(8, 28 - m)
        tiles = []
        for t in range(32):
            v = praw[m : m + rows, t * 128 : t * 128 + 128].astype(jnp.float32)
            tiles.append(v if rows == 8 else jnp.concatenate([v, v], axis=0))
        for t, v in enumerate(columns_out(tiles)):
            at = (t % 4) * 28 + m
            pf[t // 4, at : at + rows, :] = v[:rows]
    for t in range(8):
        pt[t] = pf[t].astype(jnp.bfloat16)
    pall[q, j] = pt[j]
    pl.semaphore_wait(barrier, 11)

    remote(pt.at[partner], pall.at[q, j], zs, zr.at[0], in_column(partner)).start()
    for e in (1, 3, 2):
        for c in (0, 1):
            t = 2 * m4(z - e) + c
            remote(pt.at[t], pall.at[q, j], zs, zr.at[e], in_column(t)).start()

    def lead(e):
        return 0 if e in (0, 3) else 1

    def spot(e, aoff, boff, rows):
        if lead(e) == 0:
            n = ys[boff] * 4 + xs[aoff]
        else:
            n = ys[aoff] * 4 + xs[boff]
        return pall.at[n, pl.ds(2 * chip[e] + rows[0], rows[1])]

    def send(e, sem, aoff, boff, rows, axis, step):
        ref = spot(e, aoff, boff, rows)
        to = beside[(lead(e) if axis == "a" else 1 - lead(e), step)]
        remote(ref, ref, ss, sem, to).start()

    def both(e, ident, aoff):
        send(e, rs.at[e, ident], aoff, 0, ALL, "b", 1)
        send(e, rs.at[e, ident + 1], aoff, 0, ALL, "b", -1)

    def first(e):
        if e == 0:
            take(pall.at[q, partner], zr.at[0])
        else:
            take(pall.at[q, pl.ds(2 * chip[e], 2)], zr.at[e])
        send(e, rs.at[e, 0], 0, 0, ALL, "a", 1)
        send(e, rs.at[e, 1], 0, 0, ALL, "a", -1)
        both(e, 4, 0)

    def second(e):
        take(spot(e, -1, 0, ALL), rs.at[e, 0])
        send(e, rs.at[e, 2], -1, 0, LO, "a", 1)
        both(e, 6, -1)
        take(spot(e, 1, 0, ALL), rs.at[e, 1])
        send(e, rs.at[e, 2], 1, 0, HI, "a", -1)
        both(e, 8, 1)

    def opposite(e):
        take(spot(e, 2, 0, ALL), rs.at[e, 2])
        both(e, 10, 2)

    def onward(e, aoff):
        i = ORDER[aoff]
        take(spot(e, aoff, -1, ALL), rs.at[e, 4 + 2 * i])
        send(e, rl_, aoff, -1, LO, "b", 1)
        take(spot(e, aoff, 1, ALL), rs.at[e, 5 + 2 * i])
        send(e, rl_, aoff, 1, HI, "b", -1)

    first(0)

    loads[1].wait()
    for kk in range(7):
        for t in range(32):
            af[kk, pl.ds(t, 4, stride=32), :] = araw[kk, :, t * 128 : t * 128 + 128].astype(jnp.float32)
    for kk in range(7):
        for r in range(4):
            amine[r, kk] = af[kk, 32 * r : 32 * r + 32, :].astype(jnp.bfloat16)
    loads[2].wait()
    loads[3].wait()
    none = jnp.full((4, 4), -1, jnp.int32)
    for h in (0, 1):
        pieces = []
        for kk in range(4 * h, 4 * h + 4):
            pieces += [sraw[kk], none] if kk < 7 else [craw[...], jnp.full((4, 25), -1, jnp.int32)]
        imine[h] = jnp.concatenate(pieces, axis=1)

    def a_part(t):
        return abuf.at[t % 4, pl.ds((t // 4) * 4, 4)]

    a_own = abuf.at[layer, pl.ds(half * 4, 4)]
    own = [pltpu.make_async_copy(amine, a_own, ls.at[4]), pltpu.make_async_copy(imine, ibuf.at[part_of_j], ls.at[5])]
    for c in own:
        c.start()
    a_from = {e: 2 * chip[e] + core for e in (1, 2, 3)}
    for e in (2, 1, 3):
        remote(amine, a_own, as_.at[0], ar.at[e], in_column(2 * m4(z - e) + core)).start()
    remote(amine, a_own, as_.at[1], ar.at[0], in_column(partner)).start()
    for to in targets:
        remote(imine, ibuf.at[part_of_j], is_, ir, to).start()

    def a_step(e):
        ref = a_part(a_from[e])
        take(ref, ar.at[e])
        remote(ref, ref, as_.at[1], ar.at[0], in_column(partner)).start()

    for e in QUARTERS[1:]:
        first(e)
    for l in range(4):
        base = l * 256 + 224
        prod_hi[base : base + 32, :] = jnp.zeros((32, 512), jnp.bfloat16)
        prod_lo[base : base + 32, :] = jnp.zeros((32, 512), jnp.bfloat16)
    for e in QUARTERS:
        second(e)
    for e in QUARTERS:
        onward(e, 0)
    take(ibuf.at[pl.ds(0, 7)], ir)
    for c in own:
        c.wait()
    cols = pltpu.make_async_copy(ibuf.at[:, 1], csm, smem_sem)
    cols.start()

    target = lax.broadcasted_iota(jnp.int32, (128, 256), 0)

    def choose(r, carry):
        for l in range(4):
            s = [ibuf[l * 2 + r // 4, h, pl.ds(r % 4, 1)] for h in (0, 1)]
            lanes = jnp.concatenate(s, axis=1)
            oh[r, l] = jnp.where(lanes == target, 1.0, 0.0).astype(jnp.bfloat16)
        for n, e in enumerate(QUARTERS):
            pl.when(r == 2 * n)(lambda e=e: opposite(e))
        return carry

    lax.fori_loop(0, 8, choose, 0)
    for e in QUARTERS:
        onward(e, -1)
    for e in QUARTERS:
        onward(e, 1)
    a_step(1)
    a_step(3)
    a_step(2)
    for e in QUARTERS:
        onward(e, 2)

    left = lax.broadcasted_iota(jnp.int32, (64, 128), 1) < 64

    def weigh(r):
        for l in range(4):
            for kk in range(7):
                even_odd = abuf[l, r, kk]
                odd_even = jnp.concatenate([even_odd[:, 64:], even_odd[:, :64]], axis=1)
                zero = jnp.zeros((64, 128), jnp.bfloat16)
                wbuf[l, kk, 0:64] = jnp.where(left, jnp.concatenate([even_odd, odd_even], axis=0), zero)
                wbuf[l, kk, 64:128] = jnp.where(left, zero, jnp.concatenate([odd_even, even_odd], axis=0))

    cols.wait()

    def row_product(r):
        rh, rl = r // 4, r % 4
        for l in range(4):
            for kk in range(7):
                col = csm[l * 2 + rh, rl, 96 + kk]
                prod = lax.dot_general(
                    pall[col // 8, col % 8], wbuf[l, kk], (((1,), (1,)), ((), ())),
                    preferred_element_type=jnp.float32,
                )
                moved = pltpu.roll(prod, ROWS - 4, 0)
                base = l * 256 + kk * 32
                for cp in range(4):
                    part = prod[28 * cp : 28 * cp + 32] if cp % 2 == 0 else moved[28 * cp - 4 : 28 * cp + 28]
                    hi = part.astype(jnp.bfloat16)
                    lo = (part - hi.astype(jnp.float32)).astype(jnp.bfloat16)
                    prod_hi[base : base + 32, cp * 128 : cp * 128 + 128] = hi
                    prod_lo[base : base + 32, cp * 128 : cp * 128 + 128] = lo
        total = jnp.zeros((128, 512), jnp.float32)
        for l in range(4):
            total += jnp.dot(oh[r, l], prod_hi[l * 256 : l * 256 + 256], preferred_element_type=jnp.float32)
            total += jnp.dot(oh[r, l], prod_lo[l * 256 : l * 256 + 256], preferred_element_type=jnp.float32)
        for cp in range(4):
            turned = total[:, cp * 128 : cp * 128 + 128].T
            for c0 in (0, 1):
                for a0 in (0, 1):
                    n = 64 * c0 + 32 * a0
                    of[pl.ds(8 * a0 + 2 * cp + c0, 32, stride=16), :] = turned[n : n + 32]
        return of[...].reshape(64, 8, 128).astype(jnp.bfloat16)

    def turn(n):
        p = n // 2
        e = (2 + 2 * (p // 2) + (p // 2 + p) % 2) % 4
        return 2 * ((z + e) % 4) + (core + 1 + n) % 2

    def one_row(n, carry):
        r = turn(n)
        obuf[n] = row_product(r)

        @pl.when(n < 7)
        def _():
            remote(obuf.at[n], out.at[:, j], os, orr, in_column(r)).start()
            weigh(turn(n + 1))

        return carry

    take(abuf.at[pl.ds(0, 2)], ar.at[0])
    weigh(turn(0))
    take(pall.at[pl.ds(0, 4)], rl_)
    lax.fori_loop(0, 8, one_row, 0)
    last = pltpu.make_async_copy(obuf.at[7], out.at[:, j], smem_sem)
    last.start()

    take(pall.at[q, pl.ds(0, 7)], zs)
    take(abuf.at[pl.ds(0, 3), pl.ds(0, 4)], as_.at[0])
    take(abuf.at[pl.ds(0, 2)], as_.at[1])
    take(ibuf.at[pl.ds(0, 7)], is_)
    take(pall.at[pl.ds(0, 15)], ss)
    take(obuf.at[pl.ds(0, 7)], os)
    take(out.at[:, pl.ds(0, 7)], orr)
    last.wait()


def per_device(a_blocks, a_cols, p_blocks, slots):
    dma = pltpu.SemaphoreType.DMA
    hbm = pl.BlockSpec(memory_space=pltpu.HBM)
    got = pl.pallas_call(
        kernel,
        out_shape=jax.ShapeDtypeStruct((64, 8, 8, 128), jnp.bfloat16),
        in_specs=[hbm, hbm, hbm, hbm],
        out_specs=hbm,
        scratch_shapes=[
            pltpu.VMEM((28, 4096), jnp.bfloat16),
            pltpu.VMEM((7, 4, 4096), jnp.bfloat16),
            pltpu.VMEM((7, 4, 28), jnp.int32),
            pltpu.VMEM((4, 7), jnp.int32),
            pltpu.VMEM((8, ROWS, 128), jnp.float32),
            pltpu.VMEM((8, ROWS, 128), jnp.bfloat16),
            pltpu.VMEM((7, 128, 128), jnp.float32),
            pltpu.VMEM((4, 7, 32, 128), jnp.bfloat16),
            pltpu.VMEM((2, 4, 128), jnp.int32),
            pltpu.VMEM((16, 8, ROWS, 128), jnp.bfloat16),
            pltpu.VMEM((4, 8, 7, 32, 128), jnp.bfloat16),
            pltpu.VMEM((8, 2, 4, 128), jnp.int32),
            pltpu.SMEM((8, 4, 128), jnp.int32),
            pltpu.VMEM((4, 7, 128, 128), jnp.bfloat16),
            pltpu.VMEM((8, 4, 128, 256), jnp.bfloat16),
            pltpu.VMEM((1024, 512), jnp.bfloat16),
            pltpu.VMEM((1024, 512), jnp.bfloat16),
            pltpu.VMEM((512, 128), jnp.float32),
            pltpu.VMEM((8, 64, 8, 128), jnp.bfloat16),
            dma((6,)), dma, dma((4,)), dma((2,)), dma((4,)), dma, dma,
            dma, dma((4, 12)), dma, dma, dma, dma,
        ],
        compiler_params=pltpu.CompilerParams(
            collective_id=0, has_side_effects=True, vmem_limit_bytes=60 * 2**20
        ),
        name="column_split",
    )(p_blocks[0], a_blocks.transpose(1, 0, 2), slots.transpose(1, 0, 2), a_cols)
    return got.reshape(4096, 128).T[None]


def solution(mesh):
    placed = (
        P("grid", "layer", None),
        P("grid", "layer"),
        P(("grid", "layer"), None, None),
        P("grid", "layer", None),
    )
    return jax.shard_map(
        per_device,
        mesh=mesh,
        in_specs=placed,
        out_specs=P(("grid", "layer"), None, None),
        check_vma=False,
    )
```

```python
import jax
import jax.numpy as jnp
from jax import lax
from jax.experimental import pallas as pl
from jax.experimental.pallas import tpu as pltpu
from jax.sharding import PartitionSpec as P

MESH = pl.DeviceIdType.MESH
ROWS = 112
ALL, LO, HI = (0, 2), (0, 1), (1, 1)
ORDER = {0: 0, -1: 1, 1: 2, 2: 3}
QUARTERS = (0, 1, 3, 2)


def place():
    g, l = lax.axis_index("grid"), lax.axis_index("layer")
    return g // 8, (g // 2) % 4, (g % 2) * 4 + l


def dev(y, x, j):
    return ((y * 4 + x) * 2 + j // 4, j % 4)


def m4(v):
    return lax.rem(v + 4, 4)


def columns_out(tiles):
    lane = lax.broadcasted_iota(jnp.int32, tiles[0].shape, 1)
    for i in range(5):
        d, up = 2 << i, (lane & (2 << i)) != 0
        swapped = list(tiles)
        for t in range(32):
            if not t & (1 << i):
                low, high = tiles[t], tiles[t | (1 << i)]
                swapped[t] = jnp.where(up, pltpu.roll(high, d, 1), low)
                swapped[t | (1 << i)] = jnp.where(up, high, pltpu.roll(low, 128 - d, 1))
        tiles = swapped
    top, bottom = (lane & 64) != 0, (lane & 1) != 0
    done = []
    for v in tiles:
        moved = jnp.where(top, pltpu.roll(v, 63, 1), pltpu.roll(v, 65, 1))
        done.append(jnp.where(top == bottom, v, moved))
    return done


def kernel(
    p_raw, a_raw, slot_raw, col_src, out,
    praw, araw, sraw, craw, pf, pt, af, amine, imine,
    pall, abuf, ibuf, csm, wbuf, oh, prod_hi, prod_lo, of, obuf,
    ls, zs, zr, as_, ar, is_, ir, ss, rs, rl_, os, orr, smem_sem,
):
    y, x, j = place()
    q, z, core = y * 4 + x, j // 2, j % 2
    half, layer = j // 4, j % 4
    part_of_j = layer * 2 + half
    partner = j + 1 - 2 * core
    xs = {0: x, 1: m4(x + 1), 2: m4(x + 2), -1: m4(x - 1)}
    ys = {0: y, 1: m4(y + 1), 2: m4(y + 2), -1: m4(y - 1)}
    beside = {(0, 1): dev(y, xs[1], j), (0, -1): dev(y, xs[-1], j), (1, 1): dev(ys[1], x, j), (1, -1): dev(ys[-1], x, j)}
    chip = {e: m4(z + e) for e in range(4)}

    def in_column(t):
        return (q * 2 + t // 4, t % 4)

    targets = [in_column(lax.rem(j + d, 8)) for d in range(1, 8)]
    barrier = pltpu.get_barrier_semaphore()
    for to in targets + list(beside.values()):
        pl.semaphore_signal(barrier, inc=1, device_id=to, device_id_type=MESH)
    loads = [
        pltpu.make_async_copy(p_raw, praw, ls.at[0]),
        pltpu.make_async_copy(a_raw, araw, ls.at[1]),
        pltpu.make_async_copy(slot_raw, sraw, ls.at[2]),
        pltpu.make_async_copy(col_src, craw, ls.at[3]),
    ]
    for c in loads:
        c.start()

    def remote(s, d, ssem, rsem, to):
        return pltpu.make_async_remote_copy(
            src_ref=s, dst_ref=d, send_sem=ssem, recv_sem=rsem, device_id=to, device_id_type=MESH
        )

    def take(ref, sem):
        pltpu.make_async_copy(ref, ref, sem).wait()

    loads[0].wait()
    for m in (0, 8, 16, 24):
        rows = min(8, 28 - m)
        tiles = []
        for t in range(32):
            v = praw[m : m + rows, t * 128 : t * 128 + 128].astype(jnp.float32)
            tiles.append(v if rows == 8 else jnp.concatenate([v, v], axis=0))
        for t, v in enumerate(columns_out(tiles)):
            at = (t % 4) * 28 + m
            pf[t // 4, at : at + rows, :] = v[:rows]
    for t in range(8):
        pt[t] = pf[t].astype(jnp.bfloat16)
    pall[q, j] = pt[j]
    pl.semaphore_wait(barrier, 11)

    remote(pt.at[partner], pall.at[q, j], zs, zr.at[0], in_column(partner)).start()
    for e in (1, 3, 2):
        for c in (0, 1):
            t = 2 * m4(z - e) + c
            remote(pt.at[t], pall.at[q, j], zs, zr.at[e], in_column(t)).start()

    def lead(e):
        return 0 if e in (0, 3) else 1

    def spot(e, aoff, boff, rows):
        if lead(e) == 0:
            n = ys[boff] * 4 + xs[aoff]
        else:
            n = ys[aoff] * 4 + xs[boff]
        return pall.at[n, pl.ds(2 * chip[e] + rows[0], rows[1])]

    def send(e, sem, aoff, boff, rows, axis, step):
        ref = spot(e, aoff, boff, rows)
        to = beside[(lead(e) if axis == "a" else 1 - lead(e), step)]
        remote(ref, ref, ss, sem, to).start()

    def both(e, ident, aoff):
        send(e, rs.at[e, ident], aoff, 0, ALL, "b", 1)
        send(e, rs.at[e, ident + 1], aoff, 0, ALL, "b", -1)

    def first(e):
        if e == 0:
            take(pall.at[q, partner], zr.at[0])
        else:
            take(pall.at[q, pl.ds(2 * chip[e], 2)], zr.at[e])
        send(e, rs.at[e, 0], 0, 0, ALL, "a", 1)
        send(e, rs.at[e, 1], 0, 0, ALL, "a", -1)
        both(e, 4, 0)

    def second(e):
        take(spot(e, -1, 0, ALL), rs.at[e, 0])
        send(e, rs.at[e, 2], -1, 0, LO, "a", 1)
        both(e, 6, -1)
        take(spot(e, 1, 0, ALL), rs.at[e, 1])
        send(e, rs.at[e, 2], 1, 0, HI, "a", -1)
        both(e, 8, 1)

    def opposite(e):
        take(spot(e, 2, 0, ALL), rs.at[e, 2])
        both(e, 10, 2)

    def onward(e, aoff):
        i = ORDER[aoff]
        take(spot(e, aoff, -1, ALL), rs.at[e, 4 + 2 * i])
        send(e, rl_, aoff, -1, LO, "b", 1)
        take(spot(e, aoff, 1, ALL), rs.at[e, 5 + 2 * i])
        send(e, rl_, aoff, 1, HI, "b", -1)

    first(0)

    loads[1].wait()
    for kk in range(7):
        for t in range(32):
            af[kk, pl.ds(t, 4, stride=32), :] = araw[kk, :, t * 128 : t * 128 + 128].astype(jnp.float32)
    for kk in range(7):
        for r in range(4):
            amine[r, kk] = af[kk, 32 * r : 32 * r + 32, :].astype(jnp.bfloat16)
    def a_part(t):
        return abuf.at[t % 4, pl.ds((t // 4) * 4, 4)]

    a_own = abuf.at[layer, pl.ds(half * 4, 4)]
    own = [pltpu.make_async_copy(amine, a_own, ls.at[4]), pltpu.make_async_copy(imine, ibuf.at[part_of_j], ls.at[5])]
    own[0].start()
    a_from = {e: 2 * chip[e] + core for e in (1, 2, 3)}
    for e in (2, 1, 3):
        remote(amine, a_own, as_.at[0], ar.at[e], in_column(2 * m4(z - e) + core)).start()
    remote(amine, a_own, as_.at[1], ar.at[0], in_column(partner)).start()

    def a_step(e):
        ref = a_part(a_from[e])
        take(ref, ar.at[e])
        remote(ref, ref, as_.at[1], ar.at[0], in_column(partner)).start()

    for e in QUARTERS[1:]:
        first(e)
    for l in range(4):
        base = l * 256 + 224
        prod_hi[base : base + 32, :] = jnp.zeros((32, 512), jnp.bfloat16)
        prod_lo[base : base + 32, :] = jnp.zeros((32, 512), jnp.bfloat16)
    second(0)
    second(1)
    loads[2].wait()
    loads[3].wait()
    none = jnp.full((4, 4), -1, jnp.int32)
    for h in (0, 1):
        pieces = []
        for kk in range(4 * h, 4 * h + 4):
            pieces += [sraw[kk], none] if kk < 7 else [craw[...], jnp.full((4, 25), -1, jnp.int32)]
        imine[h] = jnp.concatenate(pieces, axis=1)

    own[1].start()
    for to in targets:
        remote(imine, ibuf.at[part_of_j], is_, ir, to).start()
    second(3)
    second(2)
    for e in QUARTERS:
        onward(e, 0)
    take(ibuf.at[pl.ds(0, 7)], ir)
    for c in own:
        c.wait()
    cols = pltpu.make_async_copy(ibuf.at[:, 1], csm, smem_sem)
    cols.start()

    target = lax.broadcasted_iota(jnp.int32, (128, 256), 0)

    def choose(r, carry):
        for l in range(4):
            s = [ibuf[l * 2 + r // 4, h, pl.ds(r % 4, 1)] for h in (0, 1)]
            lanes = jnp.concatenate(s, axis=1)
            oh[r, l] = jnp.where(lanes == target, 1.0, 0.0).astype(jnp.bfloat16)
        for n, e in enumerate(QUARTERS):
            pl.when(r == n)(lambda e=e: opposite(e))
            pl.when(r == n + 4)(lambda e=e: onward(e, -1))
        return carry

    lax.fori_loop(0, 8, choose, 0)
    for e in QUARTERS:
        onward(e, 1)
    a_step(1)
    a_step(3)
    a_step(2)
    for e in QUARTERS:
        onward(e, 2)

    left = lax.broadcasted_iota(jnp.int32, (64, 128), 1) < 64

    def weigh(r):
        for l in range(4):
            for kk in range(7):
                even_odd = abuf[l, r, kk]
                odd_even = jnp.concatenate([even_odd[:, 64:], even_odd[:, :64]], axis=1)
                zero = jnp.zeros((64, 128), jnp.bfloat16)
                wbuf[l, kk, 0:64] = jnp.where(left, jnp.concatenate([even_odd, odd_even], axis=0), zero)
                wbuf[l, kk, 64:128] = jnp.where(left, zero, jnp.concatenate([odd_even, even_odd], axis=0))

    cols.wait()

    def row_product(r):
        rh, rl = r // 4, r % 4
        for l in range(4):
            for kk in range(7):
                col = csm[l * 2 + rh, rl, 96 + kk]
                prod = lax.dot_general(
                    pall[col // 8, col % 8], wbuf[l, kk], (((1,), (1,)), ((), ())),
                    preferred_element_type=jnp.float32,
                )
                moved = pltpu.roll(prod, ROWS - 4, 0)
                base = l * 256 + kk * 32
                for cp in range(4):
                    part = prod[28 * cp : 28 * cp + 32] if cp % 2 == 0 else moved[28 * cp - 4 : 28 * cp + 28]
                    hi = part.astype(jnp.bfloat16)
                    lo = (part - hi.astype(jnp.float32)).astype(jnp.bfloat16)
                    prod_hi[base : base + 32, cp * 128 : cp * 128 + 128] = hi
                    prod_lo[base : base + 32, cp * 128 : cp * 128 + 128] = lo
        total = jnp.zeros((128, 512), jnp.float32)
        for l in range(4):
            total += jnp.dot(oh[r, l], prod_hi[l * 256 : l * 256 + 256], preferred_element_type=jnp.float32)
            total += jnp.dot(oh[r, l], prod_lo[l * 256 : l * 256 + 256], preferred_element_type=jnp.float32)
        for cp in range(4):
            turned = total[:, cp * 128 : cp * 128 + 128].T
            for c0 in (0, 1):
                for a0 in (0, 1):
                    n = 64 * c0 + 32 * a0
                    of[pl.ds(8 * a0 + 2 * cp + c0, 32, stride=16), :] = turned[n : n + 32]
        return of[...].reshape(64, 8, 128).astype(jnp.bfloat16)

    def turn(n):
        p = n // 2
        e = (2 + 2 * (p // 2) + (p // 2 + p) % 2) % 4
        return 2 * ((z + e) % 4) + (core + 1 + n) % 2

    def one_row(n, carry):
        r = turn(n)
        obuf[n] = row_product(r)

        @pl.when(n < 7)
        def _():
            remote(obuf.at[n], out.at[:, j], os, orr, in_column(r)).start()
            weigh(turn(n + 1))

        return carry

    take(abuf.at[pl.ds(0, 2)], ar.at[0])
    weigh(turn(0))
    take(pall.at[pl.ds(0, 4)], rl_)
    lax.fori_loop(0, 8, one_row, 0)
    last = pltpu.make_async_copy(obuf.at[7], out.at[:, j], smem_sem)
    last.start()

    take(pall.at[q, pl.ds(0, 7)], zs)
    take(abuf.at[pl.ds(0, 3), pl.ds(0, 4)], as_.at[0])
    take(abuf.at[pl.ds(0, 2)], as_.at[1])
    take(ibuf.at[pl.ds(0, 7)], is_)
    take(pall.at[pl.ds(0, 15)], ss)
    take(obuf.at[pl.ds(0, 7)], os)
    take(out.at[:, pl.ds(0, 7)], orr)
    last.wait()


def per_device(a_blocks, a_cols, p_blocks, slots):
    dma = pltpu.SemaphoreType.DMA
    hbm = pl.BlockSpec(memory_space=pltpu.HBM)
    got = pl.pallas_call(
        kernel,
        out_shape=jax.ShapeDtypeStruct((64, 8, 8, 128), jnp.bfloat16),
        in_specs=[hbm, hbm, hbm, hbm],
        out_specs=hbm,
        scratch_shapes=[
            pltpu.VMEM((28, 4096), jnp.bfloat16),
            pltpu.VMEM((7, 4, 4096), jnp.bfloat16),
            pltpu.VMEM((7, 4, 28), jnp.int32),
            pltpu.VMEM((4, 7), jnp.int32),
            pltpu.VMEM((8, ROWS, 128), jnp.float32),
            pltpu.VMEM((8, ROWS, 128), jnp.bfloat16),
            pltpu.VMEM((7, 128, 128), jnp.float32),
            pltpu.VMEM((4, 7, 32, 128), jnp.bfloat16),
            pltpu.VMEM((2, 4, 128), jnp.int32),
            pltpu.VMEM((16, 8, ROWS, 128), jnp.bfloat16),
            pltpu.VMEM((4, 8, 7, 32, 128), jnp.bfloat16),
            pltpu.VMEM((8, 2, 4, 128), jnp.int32),
            pltpu.SMEM((8, 4, 128), jnp.int32),
            pltpu.VMEM((4, 7, 128, 128), jnp.bfloat16),
            pltpu.VMEM((8, 4, 128, 256), jnp.bfloat16),
            pltpu.VMEM((1024, 512), jnp.bfloat16),
            pltpu.VMEM((1024, 512), jnp.bfloat16),
            pltpu.VMEM((512, 128), jnp.float32),
            pltpu.VMEM((8, 64, 8, 128), jnp.bfloat16),
            dma((6,)), dma, dma((4,)), dma((2,)), dma((4,)), dma, dma,
            dma, dma((4, 12)), dma, dma, dma, dma,
        ],
        compiler_params=pltpu.CompilerParams(
            collective_id=0, has_side_effects=True, vmem_limit_bytes=60 * 2**20
        ),
        name="column_split",
    )(p_blocks[0], a_blocks.transpose(1, 0, 2), slots.transpose(1, 0, 2), a_cols)
    return got.reshape(4096, 128).T[None]


def solution(mesh):
    placed = (
        P("grid", "layer", None),
        P("grid", "layer"),
        P(("grid", "layer"), None, None),
        P("grid", "layer", None),
    )
    return jax.shard_map(
        per_device,
        mesh=mesh,
        in_specs=placed,
        out_specs=P(("grid", "layer"), None, None),
        check_vma=False,
    )
```

```python
import jax
import jax.numpy as jnp
from jax import lax
from jax.experimental import pallas as pl
from jax.experimental.pallas import tpu as pltpu
from jax.sharding import PartitionSpec as P

MESH = pl.DeviceIdType.MESH
ROWS = 112
ALL, LO, HI = (0, 2), (0, 1), (1, 1)
ORDER = {0: 0, -1: 1, 1: 2, 2: 3}
QUARTERS = (0, 1, 3, 2)


def place():
    g, l = lax.axis_index("grid"), lax.axis_index("layer")
    return g // 8, (g // 2) % 4, (g % 2) * 4 + l


def dev(y, x, j):
    return ((y * 4 + x) * 2 + j // 4, j % 4)


def m4(v):
    return lax.rem(v + 4, 4)


def bit_swap(n, pairs):
    k = lax.broadcasted_iota(jnp.int32, (n, 128), 0)
    to = k
    for i, o in pairs:
        odd = ((k >> i) ^ (k >> o)) & 1
        to = to ^ (odd << i) ^ (odd << o)
    lane = lax.broadcasted_iota(jnp.int32, (n, 128), 1)
    parts = [jnp.where(to == lane + 128 * t, 1.0, 0.0).astype(jnp.bfloat16) for t in range(n // 128)]
    return jnp.concatenate(parts, axis=1)


def columns_out(tile, px):
    tiles = [tile(t) for t in range(32)]
    for high, pairs in ((3, ((8, 5), (7, 4))), (1, ((8, 3), (7, 2))), (0, ((7, 1), (6, 0)))):
        step = 1 << high
        count = 4 if high else 2
        picks = [t for t in range(32) if not t & ((count - 1) * step)]
        for i, t in enumerate(picks):
            for n in range(count):
                px[i * 32 : i * 32 + 32, n * 128 : n * 128 + 128] = tiles[t + n * step]
        moved = jnp.dot(
            px[0 : 32 * len(picks), 0 : 128 * count], bit_swap(128 * count, pairs), preferred_element_type=jnp.float32
        )
        for i, t in enumerate(picks):
            for n in range(count):
                tiles[t + n * step] = moved[i * 32 : i * 32 + 32, n * 128 : n * 128 + 128].astype(jnp.bfloat16)
    return tiles


def kernel(
    p_raw, a_raw, slot_raw, col_src, out,
    praw, araw, sraw, craw, px, pf, pt, af, amine, imine,
    pall, abuf, ibuf, csm, wbuf, oh, prod_hi, prod_lo, of, obuf,
    ls, zs, zr, as_, ar, is_, ir, ss, rs, rl_, os, orr, smem_sem,
):
    y, x, j = place()
    q, z, core = y * 4 + x, j // 2, j % 2
    half, layer = j // 4, j % 4
    part_of_j = layer * 2 + half
    partner = j + 1 - 2 * core
    xs = {0: x, 1: m4(x + 1), 2: m4(x + 2), -1: m4(x - 1)}
    ys = {0: y, 1: m4(y + 1), 2: m4(y + 2), -1: m4(y - 1)}
    beside = {(0, 1): dev(y, xs[1], j), (0, -1): dev(y, xs[-1], j), (1, 1): dev(ys[1], x, j), (1, -1): dev(ys[-1], x, j)}
    chip = {e: m4(z + e) for e in range(4)}

    def in_column(t):
        return (q * 2 + t // 4, t % 4)

    targets = [in_column(lax.rem(j + d, 8)) for d in range(1, 8)]
    barrier = pltpu.get_barrier_semaphore()
    for to in targets + list(beside.values()):
        pl.semaphore_signal(barrier, inc=1, device_id=to, device_id_type=MESH)
    loads = [
        pltpu.make_async_copy(p_raw, praw, ls.at[0]),
        pltpu.make_async_copy(a_raw, araw, ls.at[1]),
        pltpu.make_async_copy(slot_raw, sraw, ls.at[2]),
        pltpu.make_async_copy(col_src, craw, ls.at[3]),
    ]
    for c in loads:
        c.start()

    def remote(s, d, ssem, rsem, to):
        return pltpu.make_async_remote_copy(
            src_ref=s, dst_ref=d, send_sem=ssem, recv_sem=rsem, device_id=to, device_id_type=MESH
        )

    def take(ref, sem):
        pltpu.make_async_copy(ref, ref, sem).wait()

    loads[0].wait()
    def tile(t):
        v = praw[:, t * 128 : t * 128 + 128].astype(jnp.float32)
        return jnp.concatenate([v, jnp.zeros((4, 128), jnp.float32)], axis=0).astype(jnp.bfloat16)

    for t, v in enumerate(columns_out(tile, px)):
        pf[t // 4, t % 4 * 28 : t % 4 * 28 + 28, :] = v[:28].astype(jnp.float32)
    for t in range(8):
        pt[t] = pf[t].astype(jnp.bfloat16)
    pall[q, j] = pt[j]
    pl.semaphore_wait(barrier, 11)

    def lead(e):
        return 0 if e in (0, 3) else 1

    def spot(e, aoff, boff, rows):
        if lead(e) == 0:
            n = ys[boff] * 4 + xs[aoff]
        else:
            n = ys[aoff] * 4 + xs[boff]
        return pall.at[n, pl.ds(2 * chip[e] + rows[0], rows[1])]

    def send(e, sem, aoff, boff, rows, axis, step):
        ref = spot(e, aoff, boff, rows)
        to = beside[(lead(e) if axis == "a" else 1 - lead(e), step)]
        remote(ref, ref, ss, sem, to).start()

    def both(e, ident, aoff):
        send(e, rs.at[e, ident], aoff, 0, ALL, "b", 1)
        send(e, rs.at[e, ident + 1], aoff, 0, ALL, "b", -1)

    def one_row_out(row):
        ref = pall.at[q, row]
        for axis, step, ident in ((0, 1, 0), (0, -1, 1), (1, 1, 4), (1, -1, 5)):
            remote(ref, ref, ss, rs.at[0, ident], beside[(axis, step)]).start()

    def first(e):
        if e == 0:
            take(pall.at[q, partner], zr.at[0])
            one_row_out(partner)
            return
        take(pall.at[q, pl.ds(2 * chip[e], 2)], zr.at[e])
        send(e, rs.at[e, 0], 0, 0, ALL, "a", 1)
        send(e, rs.at[e, 1], 0, 0, ALL, "a", -1)
        both(e, 4, 0)

    def second(e):
        take(spot(e, -1, 0, ALL), rs.at[e, 0])
        send(e, rs.at[e, 2], -1, 0, LO, "a", 1)
        both(e, 6, -1)
        take(spot(e, 1, 0, ALL), rs.at[e, 1])
        send(e, rs.at[e, 2], 1, 0, HI, "a", -1)
        both(e, 8, 1)

    def opposite(e):
        take(spot(e, 2, 0, ALL), rs.at[e, 2])
        both(e, 10, 2)

    def onward(e, aoff):
        i = ORDER[aoff]
        take(spot(e, aoff, -1, ALL), rs.at[e, 4 + 2 * i])
        send(e, rl_, aoff, -1, LO, "b", 1)
        take(spot(e, aoff, 1, ALL), rs.at[e, 5 + 2 * i])
        send(e, rl_, aoff, 1, HI, "b", -1)

    remote(pt.at[partner], pall.at[q, j], zs, zr.at[0], in_column(partner)).start()
    one_row_out(j)
    for e in (1, 3, 2):
        for c in (0, 1):
            t = 2 * m4(z - e) + c
            remote(pt.at[t], pall.at[q, j], zs, zr.at[e], in_column(t)).start()

    first(0)

    loads[1].wait()
    for kk in range(7):
        for t in range(32):
            af[kk, pl.ds(t, 4, stride=32), :] = araw[kk, :, t * 128 : t * 128 + 128].astype(jnp.float32)
    for kk in range(7):
        for r in range(4):
            amine[r, kk] = af[kk, 32 * r : 32 * r + 32, :].astype(jnp.bfloat16)
    def a_part(t):
        return abuf.at[t % 4, pl.ds((t // 4) * 4, 4)]

    a_own = abuf.at[layer, pl.ds(half * 4, 4)]
    own = [pltpu.make_async_copy(amine, a_own, ls.at[4]), pltpu.make_async_copy(imine, ibuf.at[part_of_j], ls.at[5])]
    own[0].start()
    a_from = {e: 2 * chip[e] + core for e in (1, 2, 3)}
    for e in (2, 1, 3):
        remote(amine, a_own, as_.at[0], ar.at[e], in_column(2 * m4(z - e) + core)).start()
    remote(amine, a_own, as_.at[1], ar.at[0], in_column(partner)).start()

    def a_step(e):
        ref = a_part(a_from[e])
        take(ref, ar.at[e])
        remote(ref, ref, as_.at[1], ar.at[0], in_column(partner)).start()

    for e in QUARTERS[1:]:
        first(e)
    for l in range(4):
        base = l * 256 + 224
        prod_hi[base : base + 32, :] = jnp.zeros((32, 512), jnp.bfloat16)
        prod_lo[base : base + 32, :] = jnp.zeros((32, 512), jnp.bfloat16)
    second(0)
    second(1)
    loads[2].wait()
    loads[3].wait()
    none = jnp.full((4, 4), -1, jnp.int32)
    for h in (0, 1):
        pieces = []
        for kk in range(4 * h, 4 * h + 4):
            pieces += [sraw[kk], none] if kk < 7 else [craw[...], jnp.full((4, 25), -1, jnp.int32)]
        imine[h] = jnp.concatenate(pieces, axis=1)

    own[1].start()
    for to in targets:
        remote(imine, ibuf.at[part_of_j], is_, ir, to).start()
    second(3)
    second(2)
    for e in QUARTERS:
        onward(e, 0)
    take(ibuf.at[pl.ds(0, 7)], ir)
    for c in own:
        c.wait()
    cols = pltpu.make_async_copy(ibuf.at[:, 1], csm, smem_sem)
    cols.start()

    target = lax.broadcasted_iota(jnp.int32, (128, 256), 0)

    def choose(r, carry):
        for l in range(4):
            s = [ibuf[l * 2 + r // 4, h, pl.ds(r % 4, 1)] for h in (0, 1)]
            lanes = jnp.concatenate(s, axis=1)
            oh[r, l] = jnp.where(lanes == target, 1.0, 0.0).astype(jnp.bfloat16)
        for n, e in enumerate(QUARTERS):
            pl.when(r == n)(lambda e=e: opposite(e))
            pl.when(r == n + 4)(lambda e=e: onward(e, -1))
        return carry

    lax.fori_loop(0, 8, choose, 0)
    for e in QUARTERS:
        onward(e, 1)
    a_step(1)
    a_step(3)
    a_step(2)
    for e in QUARTERS:
        onward(e, 2)

    left = lax.broadcasted_iota(jnp.int32, (64, 128), 1) < 64

    def weigh(r):
        for l in range(4):
            for kk in range(7):
                even_odd = abuf[l, r, kk]
                odd_even = jnp.concatenate([even_odd[:, 64:], even_odd[:, :64]], axis=1)
                zero = jnp.zeros((64, 128), jnp.bfloat16)
                wbuf[l, kk, 0:64] = jnp.where(left, jnp.concatenate([even_odd, odd_even], axis=0), zero)
                wbuf[l, kk, 64:128] = jnp.where(left, zero, jnp.concatenate([odd_even, even_odd], axis=0))

    cols.wait()

    def row_product(r):
        rh, rl = r // 4, r % 4
        for l in range(4):
            for kk in range(7):
                col = csm[l * 2 + rh, rl, 96 + kk]
                prod = lax.dot_general(
                    pall[col // 8, col % 8], wbuf[l, kk], (((1,), (1,)), ((), ())),
                    preferred_element_type=jnp.float32,
                )
                moved = pltpu.roll(prod, ROWS - 4, 0)
                base = l * 256 + kk * 32
                for cp in range(4):
                    part = prod[28 * cp : 28 * cp + 32] if cp % 2 == 0 else moved[28 * cp - 4 : 28 * cp + 28]
                    hi = part.astype(jnp.bfloat16)
                    lo = (part - hi.astype(jnp.float32)).astype(jnp.bfloat16)
                    prod_hi[base : base + 32, cp * 128 : cp * 128 + 128] = hi
                    prod_lo[base : base + 32, cp * 128 : cp * 128 + 128] = lo
        total = jnp.zeros((128, 512), jnp.float32)
        for l in range(4):
            total += jnp.dot(oh[r, l], prod_hi[l * 256 : l * 256 + 256], preferred_element_type=jnp.float32)
            total += jnp.dot(oh[r, l], prod_lo[l * 256 : l * 256 + 256], preferred_element_type=jnp.float32)
        for cp in range(4):
            turned = total[:, cp * 128 : cp * 128 + 128].T
            for c0 in (0, 1):
                for a0 in (0, 1):
                    n = 64 * c0 + 32 * a0
                    of[pl.ds(8 * a0 + 2 * cp + c0, 32, stride=16), :] = turned[n : n + 32]
        return of[...].reshape(64, 8, 128).astype(jnp.bfloat16)

    def turn(n):
        p = n // 2
        e = (2 + 2 * (p // 2) + (p // 2 + p) % 2) % 4
        return 2 * ((z + e) % 4) + (core + 1 + n) % 2

    def one_row(n, carry):
        r = turn(n)
        obuf[n] = row_product(r)

        @pl.when(n < 7)
        def _():
            remote(obuf.at[n], out.at[:, j], os, orr, in_column(r)).start()
            weigh(turn(n + 1))

        return carry

    take(abuf.at[pl.ds(0, 2)], ar.at[0])
    weigh(turn(0))
    take(pall.at[pl.ds(0, 4)], rl_)
    lax.fori_loop(0, 8, one_row, 0)
    last = pltpu.make_async_copy(obuf.at[7], out.at[:, j], smem_sem)
    last.start()

    take(pall.at[q, pl.ds(0, 7)], zs)
    take(abuf.at[pl.ds(0, 3), pl.ds(0, 4)], as_.at[0])
    take(abuf.at[pl.ds(0, 2)], as_.at[1])
    take(ibuf.at[pl.ds(0, 7)], is_)
    take(pall.at[pl.ds(0, 15)], ss)
    take(obuf.at[pl.ds(0, 7)], os)
    take(out.at[:, pl.ds(0, 7)], orr)
    last.wait()


def per_device(a_blocks, a_cols, p_blocks, slots):
    dma = pltpu.SemaphoreType.DMA
    hbm = pl.BlockSpec(memory_space=pltpu.HBM)
    got = pl.pallas_call(
        kernel,
        out_shape=jax.ShapeDtypeStruct((64, 8, 8, 128), jnp.bfloat16),
        in_specs=[hbm, hbm, hbm, hbm],
        out_specs=hbm,
        scratch_shapes=[
            pltpu.VMEM((28, 4096), jnp.bfloat16),
            pltpu.VMEM((7, 4, 4096), jnp.bfloat16),
            pltpu.VMEM((7, 4, 28), jnp.int32),
            pltpu.VMEM((4, 7), jnp.int32),
            pltpu.VMEM((512, 512), jnp.bfloat16),
            pltpu.VMEM((8, ROWS, 128), jnp.float32),
            pltpu.VMEM((8, ROWS, 128), jnp.bfloat16),
            pltpu.VMEM((7, 128, 128), jnp.float32),
            pltpu.VMEM((4, 7, 32, 128), jnp.bfloat16),
            pltpu.VMEM((2, 4, 128), jnp.int32),
            pltpu.VMEM((16, 8, ROWS, 128), jnp.bfloat16),
            pltpu.VMEM((4, 8, 7, 32, 128), jnp.bfloat16),
            pltpu.VMEM((8, 2, 4, 128), jnp.int32),
            pltpu.SMEM((8, 4, 128), jnp.int32),
            pltpu.VMEM((4, 7, 128, 128), jnp.bfloat16),
            pltpu.VMEM((8, 4, 128, 256), jnp.bfloat16),
            pltpu.VMEM((1024, 512), jnp.bfloat16),
            pltpu.VMEM((1024, 512), jnp.bfloat16),
            pltpu.VMEM((512, 128), jnp.float32),
            pltpu.VMEM((8, 64, 8, 128), jnp.bfloat16),
            dma((6,)), dma, dma((4,)), dma((2,)), dma((4,)), dma, dma,
            dma, dma((4, 12)), dma, dma, dma, dma,
        ],
        compiler_params=pltpu.CompilerParams(
            collective_id=0, has_side_effects=True, vmem_limit_bytes=60 * 2**20
        ),
        name="column_split",
    )(p_blocks[0], a_blocks.transpose(1, 0, 2), slots.transpose(1, 0, 2), a_cols)
    return got.reshape(4096, 128).T[None]


def solution(mesh):
    placed = (
        P("grid", "layer", None),
        P("grid", "layer"),
        P(("grid", "layer"), None, None),
        P("grid", "layer", None),
    )
    return jax.shard_map(
        per_device,
        mesh=mesh,
        in_specs=placed,
        out_specs=P(("grid", "layer"), None, None),
        check_vma=False,
    )
```
